32 devices in a mesh: wide: 16 (over z, y, x), rows: 2 (over core).
Axes of the slice: x: 2, y: 2, z: 4, core: 2. Of those that a mesh axis runs over, the one named last changes fastest.
Arguments:
- slabs: bfloat16 [16, 2, 10, 32, 128], P('wide', 'rows'), may hold values from -6 to 6
- dest: int32 [16, 2, 10], P('wide', 'rows'), may hold values from 0 to 15, as said below
- pos: int32 [16, 2, 10], P('wide', 'rows'), may hold values from 0 to 9, as said below
- lengths: int32 [16], P('wide'), may hold values from 1 to 5
- cot: bfloat16 [16, 5, 4, 32, 128], P('wide', None, 'rows'), may hold values from -6 to 6
- w_first: bfloat16 [3456, 128], P('wide'), may hold values from -0.109375 to 0.109375
- w_second: bfloat16 [3456, 128], P('wide'), may hold values from -0.109375 to 0.109375
Outputs:
- block_out: bfloat16 [16, 5, 4, 32, 128], P('wide', None, 'rows')
- grad_input: bfloat16 [16, 5, 4, 32, 128], P('wide', None, 'rows')
- grad_w_first: float32 [3456, 128], P('wide')
- grad_w_second: float32 [3456, 128], P('wide')
The draws below stay inside these ranges and needn't reach their ends.
Inputs may be any that keep to these rules, and one draw needn't show every extreme that they name: `dest`: within a band no loader sends more than one slab to any clip; every clip receives exactly 10 slabs in each band. `pos`: for every clip and band the 10 slabs it receives carry the places 0 to 9, each once.
All inputs are finite; a program needn't handle non-finite values.
Results may differ from the reference program's by a relative error of at most 0.018.
Values may be sent and summed in bfloat16 or wider, within the bound.
No kernel may reach another device: no remote copies, remote signals or barrier semaphores. Data moves between devices by JAX's collectives and lax.ppermute only.
A program may use at most 64 MiB of HBM per device.

```python
import math
import jax
import jax.numpy as jnp
from jax import lax

C = 128
TAPS = 27
FRAMES = 5
ROWS_DEV = 2
COLS = 32
CLIPS = 16
LOADERS = 16
SLABS = 10
CAP = 1
TILE_ROWS = 4
ALL_CELLS = 10240
N_ROWS = 2


def packing_lists(key):
    shift_keys = jax.random.split(jax.random.fold_in(key, 17), N_ROWS)
    order_keys = jax.random.split(jax.random.fold_in(key, 23), N_ROWS)
    source_pool = jnp.arange(LOADERS * CAP, dtype=jnp.int32) % LOADERS
    needed = jnp.array([1, LOADERS // 2, LOADERS - 1], dtype=jnp.int32)
    half_point = LOADERS // 2
    remaining = jnp.concatenate([source_pool[0:1], source_pool[2:half_point], source_pool[half_point + 1:LOADERS - 1], source_pool[LOADERS:]])

    def pick_shifts(one_key, other_key):
        chosen = jnp.concatenate([needed, jax.random.permutation(one_key, remaining)])[:SLABS]
        return jax.random.permutation(other_key, chosen)
    shifts = jax.vmap(pick_shifts)(shift_keys, order_keys)
    loader_ids = jnp.arange(LOADERS, dtype=jnp.int32)
    destination = (loader_ids[:, None, None] + shifts[None, :, :]) % LOADERS
    place_keys = jax.random.split(jax.random.fold_in(key, 29), N_ROWS * LOADERS)

    def pick_places(one_key):
        return jax.random.permutation(one_key, SLABS).astype(jnp.int32)
    orders = jax.vmap(pick_places)(place_keys).reshape(N_ROWS, LOADERS, SLABS)
    band_ids = jnp.arange(N_ROWS, dtype=jnp.int32)[None, :, None]
    slab_ids = jnp.arange(SLABS, dtype=jnp.int32)[None, None, :]
    places = orders[band_ids, destination, slab_ids]
    return (destination.astype(jnp.int32), places.astype(jnp.int32))


def draw_dest(key, part):
    return packing_lists(key)[0]


def draw_pos(key, part):
    return packing_lists(key)[1]


def place_ends(drawn, key, low, top_value):
    spot = [jax.random.randint(jax.random.fold_in(key, axis), (), 0, length) for axis, length in enumerate(drawn.shape)]
    longest = drawn.shape.index(max(drawn.shape))
    neighbour = spot[:longest] + [(spot[longest] + 1) % drawn.shape[longest]] + spot[longest + 1:]
    return drawn.at[tuple(spot)].set(low).at[tuple(neighbour)].set(top_value)


def steps_of(key, dims, pieces, low, high):
    level = 1.0
    for dim, shards_of in pieces:
        heights = jax.random.uniform(jax.random.fold_in(jax.random.fold_in(key, 6), dim), (shards_of,), jnp.float32, low / len(pieces), high / len(pieces))
        level = level * jnp.repeat(jnp.exp(heights), dims[dim] // shards_of).reshape((-1,) + (1,) * (len(dims) - 1 - dim))
    return level


def normal_values(rng, dims, width, most, cuts=(), held_as=jnp.bfloat16):
    entries = jax.random.normal(rng, dims, jnp.float32) * width
    if len(cuts) > 0:
        entries = steps_of(rng, dims, cuts, -0.22, 0.18) * entries
    return jnp.clip(entries, min=-most, max=most).astype(held_as)


def setup_inputs(seed: int = 0) -> dict:
    splits = jax.random.split(jax.random.key(seed), 8)
    slabs = normal_values(splits[0], (LOADERS, N_ROWS, SLABS, COLS, C), 1.0, 6.0, ((0, 16), (1, 2)))
    dest = draw_dest(jax.random.fold_in(splits[7], 71), 0)
    pos = draw_pos(jax.random.fold_in(splits[7], 71), 0)
    lengths = place_ends(jax.random.randint(splits[3], (CLIPS,), 1, FRAMES + 1), jax.random.fold_in(splits[3], 1), 1, FRAMES).astype(jnp.int32)
    cot = normal_values(splits[4], (CLIPS, FRAMES, TILE_ROWS, COLS, C), 1.0, 6.0, ((0, 16), (2, 2)))
    w_first = normal_values(splits[5], (TAPS * C, C), (TAPS * C) ** -0.5, 0.109375, ((0, 16),))
    w_second = normal_values(splits[6], (TAPS * C, C), (TAPS * C) ** -0.5, 0.109375, ((0, 16),))
    return dict(slabs=slabs, dest=dest, pos=pos, lengths=lengths, cot=cot, w_first=w_first, w_second=w_second)


def silu_slope(values):
    sig = jax.nn.sigmoid(values)
    return sig * (1.0 + values * (1.0 - sig))

def causal_conv(field, kernel):
    padded = jnp.concatenate([field[:1], field[:1], field], axis=0)
    result = lax.conv_general_dilated(padded[None], kernel, (1, 1, 1), ((0, 0), (1, 1), (1, 1)), dimension_numbers=('NDHWC', 'DHWIO', 'NDHWC'), precision=lax.Precision.HIGHEST, preferred_element_type=jnp.float32)
    return result[0]

def to_bf16(values):
    rounded = values.astype(jnp.bfloat16)
    return lax.optimization_barrier(rounded).astype(jnp.float32)

def reference(slabs, dest, pos, lengths, cot, w_first, w_second):
    band_ids = jnp.arange(N_ROWS, dtype=jnp.int32)[None, :, None]
    targets = (band_ids * (CLIPS * SLABS) + dest.astype(jnp.int32) * SLABS + pos.astype(jnp.int32)).astype(jnp.int32)
    placed = jnp.zeros((N_ROWS * CLIPS * SLABS, COLS, C), jnp.bfloat16)
    placed = placed.at[targets.reshape(-1)].set(slabs.reshape(-1, COLS, C))
    placed = placed.reshape(N_ROWS, CLIPS, FRAMES, ROWS_DEV, COLS, C)
    tiles = jnp.transpose(placed, (1, 2, 0, 3, 4, 5)).reshape(CLIPS, FRAMES, TILE_ROWS, COLS, C)
    kernel_first = w_first.astype(jnp.float32).reshape(3, 3, 3, C, C)
    kernel_second = w_second.astype(jnp.float32).reshape(3, 3, 3, C, C)
    frame_ids = jnp.arange(FRAMES, dtype=jnp.int32)

    def per_clip(totals, inputs):
        tile, upstream, length = inputs
        tile_wide = tile.astype(jnp.float32)
        first = to_bf16(jax.nn.silu(tile_wide))
        act = to_bf16(causal_conv(first, kernel_first))
        second = to_bf16(jax.nn.silu(act))
        block_out = (tile_wide + causal_conv(second, kernel_second)).astype(jnp.bfloat16)
        live = (frame_ids < length)[:, None, None, None]
        out_grad = jnp.where(live, upstream.astype(jnp.float32), 0.0)
        pull_second = jax.vjp(causal_conv, second, kernel_second)[1]
        hidden_grad, weight_second = pull_second(out_grad)
        act_grad = to_bf16(hidden_grad * silu_slope(act))
        pull_first = jax.vjp(causal_conv, first, kernel_first)[1]
        first_grad, weight_first = pull_first(act_grad)
        grad_input = (out_grad + first_grad * silu_slope(tile_wide)).astype(jnp.bfloat16)
        return ((totals[0] + weight_first, totals[1] + weight_second), (block_out, grad_input))
    zeros = jnp.zeros((3, 3, 3, C, C), jnp.float32)
    totals, outputs = lax.scan(per_clip, (zeros, zeros), (tiles, cot, lengths))
    scale = 1.0 / math.sqrt(ALL_CELLS)
    grad_w_first = (totals[0] * scale).reshape(TAPS * C, C)
    grad_w_second = (totals[1] * scale).reshape(TAPS * C, C)
    return (outputs[0], outputs[1], grad_w_first, grad_w_second)
```

```python
import functools
import math

import jax
import jax.numpy as jnp
from jax import lax
from jax.experimental import pallas as pl
from jax.experimental.pallas import tpu as pltpu
from jax.sharding import PartitionSpec as P

BF16 = jnp.bfloat16
F32 = jnp.float32
LABEL_ROWS = 16


def with_halo(block, sides, width):
    for axis, dim in sides:
        count = lax.axis_size(axis)
        forward = [(i, i + 1) for i in range(count - 1)]
        backward = [(target, source) for source, target in forward]
        low = lax.ppermute(
            lax.slice_in_dim(block, block.shape[dim] - width, None, axis=dim), axis, forward
        )
        high = lax.ppermute(lax.slice_in_dim(block, 0, width, axis=dim), axis, backward)
        block = jnp.concatenate([low, block, high], axis=dim)
    return block


def silu_slope(values):
    sig = jax.nn.sigmoid(values)
    return sig * (1.0 + values * (1.0 - sig))


def conv_forward(extended, kernel):
    padded = jnp.concatenate([extended[:1], extended[:1], extended], axis=0)
    result = lax.conv_general_dilated(
        padded[None],
        kernel,
        (1, 1, 1),
        ((0, 0), (0, 0), (1, 1)),
        dimension_numbers=("NDHWC", "DHWIO", "NDHWC"),
        preferred_element_type=jnp.float32,
    )
    return result[0]


def conv_weight_grad(extended, upstream):
    padded = jnp.concatenate([extended[:1], extended[:1], extended], axis=0)
    result = lax.conv_general_dilated(
        padded[None],
        upstream[None],
        (1, 1, 1),
        ((0, 0), (0, 0), (1, 1)),
        dimension_numbers=("CDHWN", "IDHWO", "NDHWC"),
        preferred_element_type=jnp.float32,
    )
    channels = extended.shape[-1]
    return jnp.transpose(result, (1, 2, 3, 0, 4)).reshape(27 * channels, upstream.shape[-1])


def conv_data_grad(upstream_ext, kernel):
    padded = jnp.pad(upstream_ext, ((2, 2), (0, 0), (0, 0), (0, 0)))
    flipped = kernel[::-1, ::-1, ::-1]
    result = lax.conv_general_dilated(
        padded[None],
        flipped,
        (1, 1, 1),
        ((0, 0), (0, 0), (1, 1)),
        dimension_numbers=("NDHWC", "DHWOI", "NDHWC"),
        preferred_element_type=jnp.float32,
    )[0]
    head = (result[0] + result[1] + result[2])[None]
    return jnp.concatenate([head, result[3:]], axis=0)


def body_general(slabs, dest, pos, lengths, cot, w_first, w_second):
    wide_size = lax.axis_size("wide")
    band_count = lax.axis_size("rows")
    slab_count = slabs.shape[2]
    columns = slabs.shape[3]
    channels = slabs.shape[4]
    frames = cot.shape[1]
    band_rows = cot.shape[2]
    capacity = -(-slab_count // wide_size)
    slot_count = wide_size * capacity
    targets = dest[0, 0]
    places = pos[0, 0]
    ranking = jnp.arange(slab_count, dtype=jnp.int32)
    earlier = (targets[None, :] == targets[:, None]) & (ranking[None, :] < ranking[:, None])
    slab_rank = jnp.sum(earlier.astype(jnp.int32), axis=1)
    slot_of = targets * capacity + slab_rank
    placing = slot_of[None, :] == jnp.arange(slot_count, dtype=jnp.int32)[:, None]
    flat_slabs = slabs[0, 0].reshape(slab_count, columns * channels)
    outgoing = jnp.dot(placing.astype(jnp.bfloat16), flat_slabs, preferred_element_type=jnp.float32)
    outgoing = outgoing.astype(jnp.bfloat16).reshape(wide_size, capacity, columns * channels)
    labels = jnp.sum(jnp.where(placing, places[None, :] + 1, 0), axis=1) - 1
    labels = labels.reshape(wide_size, capacity)
    arrived, arrived_places = (
        lax.all_to_all(outgoing, "wide", split_axis=0, concat_axis=0, tiled=True),
        lax.all_to_all(labels, "wide", split_axis=0, concat_axis=0, tiled=True),
    )
    settle = (
        arrived_places.reshape(slot_count)[None, :]
        == jnp.arange(slab_count, dtype=jnp.int32)[:, None]
    )
    tile = jnp.dot(
        settle.astype(jnp.bfloat16),
        arrived.reshape(slot_count, columns * channels),
        preferred_element_type=jnp.float32,
    )
    tile = tile.astype(jnp.bfloat16).reshape(frames, band_rows, columns, channels)
    full_first, full_second = (
        lax.all_gather(w_first, "wide", axis=0, tiled=True),
        lax.all_gather(w_second, "wide", axis=0, tiled=True),
    )
    kernel_first = full_first.reshape(3, 3, 3, channels, channels)
    kernel_second = full_second.reshape(3, 3, 3, channels, channels)
    tile_wide = tile.astype(jnp.float32)
    first = jax.nn.silu(tile_wide).astype(jnp.bfloat16)
    first_ext = with_halo(first, (("rows", 1),), 1)
    act = conv_forward(first_ext, kernel_first).astype(jnp.bfloat16)
    second = jax.nn.silu(act.astype(jnp.float32)).astype(jnp.bfloat16)
    second_ext = with_halo(second, (("rows", 1),), 1)
    block_out = (tile_wide + conv_forward(second_ext, kernel_second)).astype(jnp.bfloat16)
    live = (jnp.arange(frames, dtype=jnp.int32) < lengths[0])[:, None, None, None]
    out_grad = jnp.where(live, cot[0], jnp.zeros_like(cot[0]))
    out_grad_ext = with_halo(out_grad, (("rows", 1),), 1)
    weight_second = conv_weight_grad(second_ext, out_grad)
    hidden_grad = conv_data_grad(out_grad_ext, kernel_second)
    act_grad = (hidden_grad * silu_slope(act.astype(jnp.float32))).astype(jnp.bfloat16)
    act_grad_ext = with_halo(act_grad, (("rows", 1),), 1)
    weight_first = conv_weight_grad(first_ext, act_grad)
    first_grad = conv_data_grad(act_grad_ext, kernel_first)
    grad_input = (out_grad.astype(jnp.float32) + first_grad * silu_slope(tile_wide)).astype(
        jnp.bfloat16
    )
    scale = 1.0 / math.sqrt(frames * band_rows * columns * band_count * wide_size)
    weight_first = weight_first * scale
    weight_second = weight_second * scale
    total_first, total_second = (
        lax.psum(weight_first.astype(jnp.bfloat16), "rows").astype(jnp.float32),
        lax.psum(weight_second.astype(jnp.bfloat16), "rows").astype(jnp.float32),
    )
    share_first, share_second = (
        lax.psum_scatter(total_first, "wide", scatter_dimension=0, tiled=True),
        lax.psum_scatter(total_second, "wide", scatter_dimension=0, tiled=True),
    )
    return (block_out[None], grad_input[None], share_first, share_second)


def pack_kernel(dest_ref, pos_ref, slabs_ref, out_ref):
    slots, rows, channels = out_ref.shape
    columns = slabs_ref.shape[1]
    out_ref[...] = jnp.zeros(out_ref.shape, BF16)
    for slot in range(slots):
        out_ref[slot, columns:, :] = jnp.full((rows - columns, channels), -1.0, BF16)
    for slab in range(slabs_ref.shape[0]):
        slot = dest_ref[slab]
        out_ref[slot, :columns, :] = slabs_ref[slab]
        place = pos_ref[slab].astype(F32)
        out_ref[slot, columns:, :] = jnp.full((rows - columns, channels), place, F32).astype(BF16)


def pack(slabs, dest, pos, slots):
    count, columns, channels = slabs.shape
    smem = pl.BlockSpec(memory_space=pltpu.SMEM)
    vmem = pl.BlockSpec(memory_space=pltpu.VMEM)
    return pl.pallas_call(
        pack_kernel,
        out_shape=jax.ShapeDtypeStruct((slots, columns + LABEL_ROWS, channels), BF16),
        in_specs=[smem, smem, vmem],
        out_specs=vmem,
    )(dest, pos, slabs)


def settle(mine, tile_ref, first_row):
    slots, rows, channels = mine.shape
    columns = rows - LABEL_ROWS
    frames = tile_ref.shape[0]
    labels = [mine[j, columns : columns + 8, :].astype(F32)[None] for j in range(slots)]
    for place in range(frames * 2):
        total = jnp.zeros((columns // 8, 8, channels), F32)
        for j in range(slots):
            values = mine[j, :columns, :].astype(F32).reshape(columns // 8, 8, channels)
            total = total + jnp.where(labels[j] == float(place), values, 0.0)
        tile_ref[place // 2, first_row + place % 2] = total.reshape(columns, channels)


def shifted(field):
    shape = field.shape
    column = lax.broadcasted_iota(jnp.int32, shape, len(shape) - 2)
    count = shape[-2]
    flat = field.reshape(-1, shape[-1])
    low = pltpu.roll(flat, 1, 0).reshape(shape)
    high = pltpu.roll(flat, flat.shape[0] - 1, 0).reshape(shape)
    low = jnp.where(column == 0, 0.0, low)
    high = jnp.where(column == count - 1, 0.0, high)
    return low.astype(BF16), field.astype(BF16), high.astype(BF16)


def spread(field, store, flip):
    rows = field.shape[1]
    columns = shifted(field)
    for b in range(3):
        for e in range(3):
            source = columns[2 - e] if flip else columns[e]
            offset = (1 - b) if flip else (b - 1)
            low = max(0, -offset)
            high = min(rows, rows - offset)
            piece = b * 3 + e
            store(low, high, piece, source[:, low + offset : high + offset])
            for row in range(rows):
                if not low <= row < high:
                    store(row, row + 1, piece, jnp.zeros_like(source[:, :1]))


def unit_kernel(
    core_ref,
    length_ref,
    mine_ref,
    other_ref,
    cot_mine_ref,
    cot_other_ref,
    w_mine_ref,
    w_other_ref,
    block_ref,
    grad_ref,
    weight_ref,
    w_scratch,
    wl_scratch,
    tile_scratch,
    act_scratch,
    x_scratch,
    g_scratch,
    up_scratch,
    sum_scratch,
    sem,
    *,
    scale,
):
    core = core_ref[0]
    length = length_ref[0]
    frames, rows, columns, channels = tile_scratch.shape
    band_rows = block_ref.shape[1]
    cells = frames * rows * columns
    nine = 9 * channels
    my_row = core * band_rows
    other_row = (1 - core) * band_rows

    load_mine = pltpu.make_async_copy(w_mine_ref, w_scratch.at[core], sem.at[0])
    load_other = pltpu.make_async_copy(w_other_ref, w_scratch.at[1 - core], sem.at[1])
    load_mine.start()
    load_other.start()

    settle(mine_ref, tile_scratch, my_row)
    settle(other_ref, tile_scratch, other_row)

    tile = tile_scratch[...]
    first = tile / (1.0 + jnp.exp(-tile))

    def store_x(index):
        def store(low, high, piece, values):
            lanes = slice(piece * channels, (piece + 1) * channels)
            x_scratch[index, 2:, low:high, :, lanes] = values
            x_scratch[index, 0, low:high, :, lanes] = values[0]
            x_scratch[index, 1, low:high, :, lanes] = values[0]

        return store

    def store_g(low, high, piece, values):
        lanes = slice(piece * channels, (piece + 1) * channels)
        g_scratch[:, low:high, :, lanes] = values

    spread(first, store_x(0), False)

    for t in range(frames):
        keep = t < length
        up_scratch[1, t, pl.ds(my_row, band_rows)] = jnp.where(
            keep, cot_mine_ref[t].astype(F32), 0.0
        ).astype(BF16)
        up_scratch[1, t, pl.ds(other_row, band_rows)] = jnp.where(
            keep, cot_other_ref[t].astype(F32), 0.0
        ).astype(BF16)

    load_mine.wait()
    load_other.wait()

    act = jnp.zeros((cells, channels), F32)
    for a in range(3):
        act = act + jnp.dot(
            x_scratch[0, a : a + frames].reshape(cells, nine),
            w_scratch[0, a].reshape(nine, channels),
            preferred_element_type=F32,
        )
    act = act.astype(BF16).reshape(frames, rows, columns, channels)
    act_scratch[...] = act
    act = act.astype(F32)
    second = act / (1.0 + jnp.exp(-act))
    spread(second, store_x(1), False)

    for index in range(2):
        for a in range(3):
            for piece in range(9):
                wl_scratch[index, a, :, piece * channels : (piece + 1) * channels] = w_scratch[
                    index, a, piece
                ]

    out_grad = up_scratch[1].astype(F32)
    spread(out_grad, store_g, True)
    nt = (((1,), (1,)), ((), ()))
    sum_scratch[...] = jnp.zeros(sum_scratch.shape, F32)
    for a in range(3):
        part = lax.dot_general(
            g_scratch[...].reshape(cells, nine),
            wl_scratch[1, a],
            nt,
            preferred_element_type=F32,
        )
        sum_scratch[a : a + frames] += part.reshape(frames, rows, columns, channels)
    sum_scratch[2] = sum_scratch[0] + sum_scratch[1] + sum_scratch[2]
    act = act_scratch[...].astype(F32)
    sig = 1.0 / (1.0 + jnp.exp(-act))
    act_grad = (sum_scratch[2:] * (sig * (1.0 + act * (1.0 - sig)))).astype(BF16)
    up_scratch[0] = act_grad

    upstream = up_scratch[core].reshape(cells, channels).astype(F32).T.astype(BF16)
    for a in range(3):
        part = jnp.dot(
            upstream,
            x_scratch[core, a : a + frames].reshape(cells, nine),
            preferred_element_type=F32,
        )
        for piece in range(9):
            weight_ref[a, piece] = (
                part[:, piece * channels : (piece + 1) * channels].T * scale
            ).astype(BF16)

    half = frames * band_rows * columns
    band = (frames, band_rows, columns, channels)
    out = jnp.zeros((half, channels), F32)
    for a in range(3):
        out = out + jnp.dot(
            x_scratch[1, a : a + frames, pl.ds(my_row, band_rows)].reshape(half, nine),
            w_scratch[1, a].reshape(nine, channels),
            preferred_element_type=F32,
        )
    my_tile = tile_scratch[:, pl.ds(my_row, band_rows)]
    block_ref[...] = (my_tile + out.reshape(band)).astype(BF16)

    spread(act_grad.astype(F32), store_g, True)
    sum_scratch[:, :band_rows] = jnp.zeros((sum_scratch.shape[0],) + band[1:], F32)
    for a in range(3):
        part = lax.dot_general(
            g_scratch[:, pl.ds(my_row, band_rows)].reshape(half, nine),
            wl_scratch[0, a],
            nt,
            preferred_element_type=F32,
        )
        sum_scratch[a : a + frames, :band_rows] += part.reshape(band)
    sum_scratch[2, :band_rows] = (
        sum_scratch[0, :band_rows] + sum_scratch[1, :band_rows] + sum_scratch[2, :band_rows]
    )
    sig = 1.0 / (1.0 + jnp.exp(-my_tile))
    slope = sig * (1.0 + my_tile * (1.0 - sig))
    my_up = up_scratch[1, :, pl.ds(my_row, band_rows)].astype(F32)
    grad_ref[...] = (my_up + sum_scratch[2:, :band_rows] * slope).astype(BF16)


def unit(core, length, mine, other, cot_mine, cot_other, w_mine, w_other, scale):
    frames, band_rows, columns, channels = cot_mine.shape
    rows = 2 * band_rows
    smem = pl.BlockSpec(memory_space=pltpu.SMEM)
    vmem = pl.BlockSpec(memory_space=pltpu.VMEM)
    hbm = pl.BlockSpec(memory_space=pl.ANY)
    band = jax.ShapeDtypeStruct(cot_mine.shape, BF16)
    flops = 2 * 27 * channels * channels * frames * rows * columns * 4
    return pl.pallas_call(
        functools.partial(unit_kernel, scale=scale),
        out_shape=(band, band, jax.ShapeDtypeStruct((3, 9, channels, channels), BF16)),
        in_specs=[smem, smem, vmem, vmem, vmem, vmem, hbm, hbm],
        out_specs=(vmem, vmem, vmem),
        scratch_shapes=[
            pltpu.VMEM((2, 3, 9, channels, channels), BF16),
            pltpu.VMEM((2, 3, channels, 9 * channels), BF16),
            pltpu.VMEM((frames, rows, columns, channels), F32),
            pltpu.VMEM((frames, rows, columns, channels), BF16),
            pltpu.VMEM((2, frames + 2, rows, columns, 9 * channels), BF16),
            pltpu.VMEM((frames, rows, columns, 9 * channels), BF16),
            pltpu.VMEM((2, frames, rows, columns, channels), BF16),
            pltpu.VMEM((frames + 2, rows, columns, channels), F32),
            pltpu.SemaphoreType.DMA((2,)),
        ],
        compiler_params=pltpu.CompilerParams(vmem_limit_bytes=40 * 1024 * 1024),
        cost_estimate=pl.CostEstimate(flops=flops, bytes_accessed=4_000_000, transcendentals=0),
    )(core, length, mine, other, cot_mine, cot_other, w_mine, w_other)


def body_pair(slabs, dest, pos, lengths, cot, w_first, w_second):
    wide_size = lax.axis_size("wide")
    core = lax.axis_index("rows")
    frames, band_rows, columns, channels = cot.shape[1:]
    share = w_first.shape[0]
    swap = [(0, 1), (1, 0)]

    def exchange(block):
        return lax.ppermute(block, "rows", swap)

    cot_mine = cot[0]
    cot_other = exchange(cot_mine)
    own = jnp.where(core == 0, w_first, w_second)
    copies = jnp.broadcast_to(own[None], (wide_size, share, channels))
    w_mine = lax.all_to_all(copies, "wide", split_axis=0, concat_axis=0, tiled=True)
    w_mine = w_mine.reshape(3, 9, channels, channels)
    w_other = exchange(w_mine)

    outgoing = pack(slabs[0, 0], dest[0, 0], pos[0, 0], wide_size)
    mine = lax.all_to_all(outgoing, "wide", split_axis=0, concat_axis=0, tiled=True)
    other = exchange(mine)

    scale = 1.0 / math.sqrt(frames * band_rows * columns * 2 * wide_size)
    block_out, grad_input, weight = unit(
        core.astype(jnp.int32).reshape(1),
        lengths,
        mine,
        other,
        cot_mine,
        cot_other,
        w_mine,
        w_other,
        scale,
    )
    parts = weight.reshape(wide_size, share, channels)
    parts = lax.all_to_all(parts, "wide", split_axis=0, concat_axis=0, tiled=True)
    total = jnp.sum(parts.astype(F32), axis=0)
    total_other = exchange(total)
    share_first = jnp.where(core == 0, total, total_other)
    share_second = jnp.where(core == 0, total_other, total)
    return (block_out[None], grad_input[None], share_first, share_second)


def solution(mesh):
    body = body_pair if mesh.shape["rows"] == 2 else body_general
    return jax.shard_map(
        body,
        mesh=mesh,
        in_specs=(
            P("wide", "rows", None, None, None),
            P("wide", "rows", None),
            P("wide", "rows", None),
            P("wide"),
            P("wide", None, "rows", None, None),
            P("wide", None),
            P("wide", None),
        ),
        out_specs=(
            P("wide", None, "rows", None, None),
            P("wide", None, "rows", None, None),
            P("wide", None),
            P("wide", None),
        ),
        check_vma=False,
    )
```

```python
import functools
import math

import jax
import jax.numpy as jnp
from jax import lax
from jax.experimental import pallas as pl
from jax.experimental.pallas import tpu as pltpu
from jax.sharding import PartitionSpec as P

BF16 = jnp.bfloat16
F32 = jnp.float32
LABEL_ROWS = 16


def with_halo(block, sides, width):
    for axis, dim in sides:
        count = lax.axis_size(axis)
        forward = [(i, i + 1) for i in range(count - 1)]
        backward = [(target, source) for source, target in forward]
        low = lax.ppermute(
            lax.slice_in_dim(block, block.shape[dim] - width, None, axis=dim), axis, forward
        )
        high = lax.ppermute(lax.slice_in_dim(block, 0, width, axis=dim), axis, backward)
        block = jnp.concatenate([low, block, high], axis=dim)
    return block


def silu_slope(values):
    sig = jax.nn.sigmoid(values)
    return sig * (1.0 + values * (1.0 - sig))


def conv_forward(extended, kernel):
    padded = jnp.concatenate([extended[:1], extended[:1], extended], axis=0)
    result = lax.conv_general_dilated(
        padded[None],
        kernel,
        (1, 1, 1),
        ((0, 0), (0, 0), (1, 1)),
        dimension_numbers=("NDHWC", "DHWIO", "NDHWC"),
        preferred_element_type=jnp.float32,
    )
    return result[0]


def conv_weight_grad(extended, upstream):
    padded = jnp.concatenate([extended[:1], extended[:1], extended], axis=0)
    result = lax.conv_general_dilated(
        padded[None],
        upstream[None],
        (1, 1, 1),
        ((0, 0), (0, 0), (1, 1)),
        dimension_numbers=("CDHWN", "IDHWO", "NDHWC"),
        preferred_element_type=jnp.float32,
    )
    channels = extended.shape[-1]
    return jnp.transpose(result, (1, 2, 3, 0, 4)).reshape(27 * channels, upstream.shape[-1])


def conv_data_grad(upstream_ext, kernel):
    padded = jnp.pad(upstream_ext, ((2, 2), (0, 0), (0, 0), (0, 0)))
    flipped = kernel[::-1, ::-1, ::-1]
    result = lax.conv_general_dilated(
        padded[None],
        flipped,
        (1, 1, 1),
        ((0, 0), (0, 0), (1, 1)),
        dimension_numbers=("NDHWC", "DHWOI", "NDHWC"),
        preferred_element_type=jnp.float32,
    )[0]
    head = (result[0] + result[1] + result[2])[None]
    return jnp.concatenate([head, result[3:]], axis=0)


def body_general(slabs, dest, pos, lengths, cot, w_first, w_second):
    wide_size = lax.axis_size("wide")
    band_count = lax.axis_size("rows")
    slab_count = slabs.shape[2]
    columns = slabs.shape[3]
    channels = slabs.shape[4]
    frames = cot.shape[1]
    band_rows = cot.shape[2]
    capacity = -(-slab_count // wide_size)
    slot_count = wide_size * capacity
    targets = dest[0, 0]
    places = pos[0, 0]
    ranking = jnp.arange(slab_count, dtype=jnp.int32)
    earlier = (targets[None, :] == targets[:, None]) & (ranking[None, :] < ranking[:, None])
    slab_rank = jnp.sum(earlier.astype(jnp.int32), axis=1)
    slot_of = targets * capacity + slab_rank
    placing = slot_of[None, :] == jnp.arange(slot_count, dtype=jnp.int32)[:, None]
    flat_slabs = slabs[0, 0].reshape(slab_count, columns * channels)
    outgoing = jnp.dot(placing.astype(jnp.bfloat16), flat_slabs, preferred_element_type=jnp.float32)
    outgoing = outgoing.astype(jnp.bfloat16).reshape(wide_size, capacity, columns * channels)
    labels = jnp.sum(jnp.where(placing, places[None, :] + 1, 0), axis=1) - 1
    labels = labels.reshape(wide_size, capacity)
    arrived, arrived_places = (
        lax.all_to_all(outgoing, "wide", split_axis=0, concat_axis=0, tiled=True),
        lax.all_to_all(labels, "wide", split_axis=0, concat_axis=0, tiled=True),
    )
    settle = (
        arrived_places.reshape(slot_count)[None, :]
        == jnp.arange(slab_count, dtype=jnp.int32)[:, None]
    )
    tile = jnp.dot(
        settle.astype(jnp.bfloat16),
        arrived.reshape(slot_count, columns * channels),
        preferred_element_type=jnp.float32,
    )
    tile = tile.astype(jnp.bfloat16).reshape(frames, band_rows, columns, channels)
    full_first, full_second = (
        lax.all_gather(w_first, "wide", axis=0, tiled=True),
        lax.all_gather(w_second, "wide", axis=0, tiled=True),
    )
    kernel_first = full_first.reshape(3, 3, 3, channels, channels)
    kernel_second = full_second.reshape(3, 3, 3, channels, channels)
    tile_wide = tile.astype(jnp.float32)
    first = jax.nn.silu(tile_wide).astype(jnp.bfloat16)
    first_ext = with_halo(first, (("rows", 1),), 1)
    act = conv_forward(first_ext, kernel_first).astype(jnp.bfloat16)
    second = jax.nn.silu(act.astype(jnp.float32)).astype(jnp.bfloat16)
    second_ext = with_halo(second, (("rows", 1),), 1)
    block_out = (tile_wide + conv_forward(second_ext, kernel_second)).astype(jnp.bfloat16)
    live = (jnp.arange(frames, dtype=jnp.int32) < lengths[0])[:, None, None, None]
    out_grad = jnp.where(live, cot[0], jnp.zeros_like(cot[0]))
    out_grad_ext = with_halo(out_grad, (("rows", 1),), 1)
    weight_second = conv_weight_grad(second_ext, out_grad)
    hidden_grad = conv_data_grad(out_grad_ext, kernel_second)
    act_grad = (hidden_grad * silu_slope(act.astype(jnp.float32))).astype(jnp.bfloat16)
    act_grad_ext = with_halo(act_grad, (("rows", 1),), 1)
    weight_first = conv_weight_grad(first_ext, act_grad)
    first_grad = conv_data_grad(act_grad_ext, kernel_first)
    grad_input = (out_grad.astype(jnp.float32) + first_grad * silu_slope(tile_wide)).astype(
        jnp.bfloat16
    )
    scale = 1.0 / math.sqrt(frames * band_rows * columns * band_count * wide_size)
    weight_first = weight_first * scale
    weight_second = weight_second * scale
    total_first, total_second = (
        lax.psum(weight_first.astype(jnp.bfloat16), "rows").astype(jnp.float32),
        lax.psum(weight_second.astype(jnp.bfloat16), "rows").astype(jnp.float32),
    )
    share_first, share_second = (
        lax.psum_scatter(total_first, "wide", scatter_dimension=0, tiled=True),
        lax.psum_scatter(total_second, "wide", scatter_dimension=0, tiled=True),
    )
    return (block_out[None], grad_input[None], share_first, share_second)


def whole(count):
    return [pl.BlockSpec(memory_space=pltpu.VMEM)] * count


def scalars(count):
    return [pl.BlockSpec(memory_space=pltpu.SMEM)] * count


def position(side):
    core = lax.axis_index("rows")
    wide = lax.axis_index("wide")
    high, low = wide // side, lax.rem(wide, side)
    return core, high, low


def walk(core, high, low):
    return jnp.where(core == 0, high, low), jnp.where(core == 0, low, high)


def chip_of(core, p, q, side):
    high, low = walk(core, p, q)
    return high * side + low


def padded_rows(rows):
    return -(-rows // 16) * 16


def pack_kernel(dest_ref, pos_ref, slabs_ref, first_ref, second_ref, *out_refs):
    side = len(out_refs)
    core, high, low = position(side)
    p, _ = walk(core, high, low)
    count, columns, channels = slabs_ref.shape
    share = first_ref.shape[0]
    base = padded_rows(share)
    row = lax.broadcasted_iota(jnp.int32, (LABEL_ROWS, channels), 0)
    own = jnp.where(core == 0, first_ref[...].astype(F32), second_ref[...].astype(F32))
    own = jnp.concatenate([own, jnp.zeros((base - share, channels), F32)], axis=0).astype(BF16)
    slabs = [slabs_ref[s].astype(F32) for s in range(count)]
    for k in range(side):
        out_refs[k][:base, :] = own
        labels = jnp.full((LABEL_ROWS, channels), -1.0, F32)
        for q in range(side):
            target = chip_of(core, jnp.bitwise_xor(p, k), q, side)
            total = jnp.zeros((columns, channels), F32)
            place = jnp.int32(-1)
            for s in range(count):
                match = dest_ref[s] == target
                total = jnp.where(match, slabs[s], total)
                place = jnp.where(match, pos_ref[s], place)
            labels = jnp.where(row == q, place.astype(F32), labels)
            at = base + q * columns
            out_refs[k][at : at + columns, :] = total.astype(BF16)
        out_refs[k][base + side * columns :, :] = labels.astype(BF16)


def pack(dest, pos, slabs, first, second, side):
    count, columns, channels = slabs.shape
    rows = padded_rows(first.shape[0]) + side * columns + LABEL_ROWS
    return pl.pallas_call(
        pack_kernel,
        out_shape=[jax.ShapeDtypeStruct((rows, channels), BF16)] * side,
        in_specs=scalars(2) + whole(3),
        out_specs=whole(side),
    )(dest, pos, slabs, first, second)


def relay_kernel(*refs, columns, base):
    side = len(refs) // 2
    ins, outs = refs[:side], refs[side:]
    core, high, low = position(side)
    _, q = walk(core, high, low)
    channels = ins[0].shape[1]
    row = lax.broadcasted_iota(jnp.int32, (LABEL_ROWS, channels), 0)
    for j in range(side):
        target = jnp.bitwise_xor(q, j)
        start = pl.multiple_of(base + target * columns, 16)
        labels = jnp.full((LABEL_ROWS, channels), -1.0, F32)
        for k in range(side):
            outs[j][k * base : (k + 1) * base, :] = ins[k][:base, :]
            at = side * base + k * columns
            outs[j][at : at + columns, :] = ins[k][pl.ds(start, columns), :]
            theirs = ins[k][base + side * columns :, :].astype(F32)
            label = jnp.sum(jnp.where(row == target, theirs, 0.0), axis=0, keepdims=True)
            labels = jnp.where(row == k, label, labels)
        outs[j][side * (base + columns) :, :] = labels.astype(BF16)


def relay(ins, columns, base):
    side = len(ins)
    channels = ins[0].shape[1]
    rows = side * (base + columns) + LABEL_ROWS
    return pl.pallas_call(
        functools.partial(relay_kernel, columns=columns, base=base),
        out_shape=[jax.ShapeDtypeStruct((rows, channels), BF16)] * side,
        in_specs=whole(side),
        out_specs=whole(side),
    )(*ins)


def settle(blocks, tile_ref, first_row, base):
    side = len(blocks)
    frames, _, columns, channels = tile_ref.shape
    slots = []
    for block in blocks:
        labels = block[side * (base + columns) :, :].astype(F32)
        for k in range(side):
            at = side * base + k * columns
            values = block[at : at + columns, :].astype(F32)
            slots.append((labels[k : k + 1], values))
    for place in range(frames * 2):
        total = jnp.zeros((columns, channels), F32)
        for label, values in slots:
            total = total + jnp.where(label == float(place), values, 0.0)
        tile_ref[place // 2, first_row + place % 2] = total


def gather_weight(blocks, wide_ref, core, high, low, share, base):
    side = len(blocks)
    p, q = walk(core, high, low)
    for j in range(side):
        for k in range(side):
            owner = chip_of(core, jnp.bitwise_xor(p, k), jnp.bitwise_xor(q, j), side)
            start = pl.multiple_of(owner * share, 8)
            values = blocks[j][k * base : (k + 1) * base, :].astype(F32)
            wide_ref[core, pl.ds(start, share), :] = values[:share]


def shifted(field):
    shape = field.shape
    column = lax.broadcasted_iota(jnp.int32, shape, len(shape) - 2)
    count = shape[-2]
    flat = field.reshape(-1, shape[-1])
    low = pltpu.roll(flat, 1, 0).reshape(shape)
    high = pltpu.roll(flat, flat.shape[0] - 1, 0).reshape(shape)
    low = jnp.where(column == 0, 0.0, low)
    high = jnp.where(column == count - 1, 0.0, high)
    return low.astype(BF16), field.astype(BF16), high.astype(BF16)


def spread(field, store, flip):
    rows = field.shape[1]
    columns = shifted(field)
    for b in range(3):
        for e in range(3):
            source = columns[2 - e] if flip else columns[e]
            offset = (1 - b) if flip else (b - 1)
            low = max(0, -offset)
            high = min(rows, rows - offset)
            piece = b * 3 + e
            store(low, high, piece, source[:, low + offset : high + offset])
            for row in range(rows):
                if not low <= row < high:
                    store(row, row + 1, piece, jnp.zeros_like(source[:, :1]))


def unit_kernel(length_ref, *refs, scale, side, share):
    refs = list(refs)

    def take(count):
        taken = refs[:count]
        del refs[:count]
        return taken

    blocks_mine, blocks_other = take(side), take(side)
    cot_mine_ref, cot_other_ref = take(2)
    block_ref, grad_ref = take(2)
    outs = take(side)
    (
        wide_ref,
        w_scratch,
        wl_scratch,
        tile_scratch,
        act_scratch,
        x_scratch,
        g_scratch,
        up_scratch,
        sum_scratch,
    ) = refs
    core, high, low = position(side)
    length = length_ref[0]
    frames, rows, columns, channels = tile_scratch.shape
    band_rows = block_ref.shape[1]
    cells = frames * rows * columns
    nine = 9 * channels
    my_row = core * band_rows
    other_row = (1 - core) * band_rows
    base = padded_rows(share)

    settle(blocks_mine, tile_scratch, my_row, base)
    settle(blocks_other, tile_scratch, other_row, base)
    gather_weight(blocks_mine, wide_ref, core, high, low, share, base)
    gather_weight(blocks_other, wide_ref, 1 - core, high, low, share, base)
    for index in range(2):
        for a in range(3):
            for piece in range(9):
                at = (a * 9 + piece) * channels
                values = wide_ref[index, at : at + channels, :].astype(BF16)
                w_scratch[index, a, piece] = values
                wl_scratch[index, a, :, piece * channels : (piece + 1) * channels] = values

    tile = tile_scratch[...]
    first = tile / (1.0 + jnp.exp(-tile))

    def store_x(index):
        def store(low, high, piece, values):
            lanes = slice(piece * channels, (piece + 1) * channels)
            x_scratch[index, 2:, low:high, :, lanes] = values
            x_scratch[index, 0, low:high, :, lanes] = values[0]
            x_scratch[index, 1, low:high, :, lanes] = values[0]

        return store

    def store_g(low, high, piece, values):
        lanes = slice(piece * channels, (piece + 1) * channels)
        g_scratch[:, low:high, :, lanes] = values

    spread(first, store_x(0), False)

    for t in range(frames):
        keep = t < length
        up_scratch[1, t, pl.ds(my_row, band_rows)] = jnp.where(
            keep, cot_mine_ref[t].astype(F32), 0.0
        ).astype(BF16)
        up_scratch[1, t, pl.ds(other_row, band_rows)] = jnp.where(
            keep, cot_other_ref[t].astype(F32), 0.0
        ).astype(BF16)

    act = jnp.zeros((cells, channels), F32)
    for a in range(3):
        act = act + jnp.dot(
            x_scratch[0, a : a + frames].reshape(cells, nine),
            w_scratch[0, a].reshape(nine, channels),
            preferred_element_type=F32,
        )
    act = act.astype(BF16).reshape(frames, rows, columns, channels)
    act_scratch[...] = act
    act = act.astype(F32)
    second = act / (1.0 + jnp.exp(-act))
    spread(second, store_x(1), False)

    out_grad = up_scratch[1].astype(F32)
    spread(out_grad, store_g, True)
    nt = (((1,), (1,)), ((), ()))
    sum_scratch[...] = jnp.zeros(sum_scratch.shape, F32)
    for a in range(3):
        part = lax.dot_general(
            g_scratch[...].reshape(cells, nine),
            wl_scratch[1, a],
            nt,
            preferred_element_type=F32,
        )
        sum_scratch[a : a + frames] += part.reshape(frames, rows, columns, channels)
    sum_scratch[2] = sum_scratch[0] + sum_scratch[1] + sum_scratch[2]
    act = act_scratch[...].astype(F32)
    sig = 1.0 / (1.0 + jnp.exp(-act))
    act_grad = (sum_scratch[2:] * (sig * (1.0 + act * (1.0 - sig)))).astype(BF16)
    up_scratch[0] = act_grad

    upstream = up_scratch[core].reshape(cells, channels).astype(F32).T.astype(BF16)
    for a in range(3):
        part = jnp.dot(
            upstream,
            x_scratch[core, a : a + frames].reshape(cells, nine),
            preferred_element_type=F32,
        )
        for piece in range(9):
            at = (a * 9 + piece) * channels
            wide_ref[0, at : at + channels, :] = (
                part[:, piece * channels : (piece + 1) * channels].T * scale
            )
    p, q = walk(core, high, low)
    for k in range(side):
        for j in range(side):
            owner = chip_of(core, j, jnp.bitwise_xor(q, k), side)
            start = pl.multiple_of(owner * share, 8)
            outs[k][j] = wide_ref[0, pl.ds(start, share), :].astype(BF16)

    half = frames * band_rows * columns
    band = (frames, band_rows, columns, channels)
    out = jnp.zeros((half, channels), F32)
    for a in range(3):
        out = out + jnp.dot(
            x_scratch[1, a : a + frames, pl.ds(my_row, band_rows)].reshape(half, nine),
            w_scratch[1, a].reshape(nine, channels),
            preferred_element_type=F32,
        )
    my_tile = tile_scratch[:, pl.ds(my_row, band_rows)]
    block_ref[...] = (my_tile + out.reshape(band)).astype(BF16)

    spread(act_grad.astype(F32), store_g, True)
    sum_scratch[:, :band_rows] = jnp.zeros((sum_scratch.shape[0],) + band[1:], F32)
    for a in range(3):
        part = lax.dot_general(
            g_scratch[:, pl.ds(my_row, band_rows)].reshape(half, nine),
            wl_scratch[0, a],
            nt,
            preferred_element_type=F32,
        )
        sum_scratch[a : a + frames, :band_rows] += part.reshape(band)
    sum_scratch[2, :band_rows] = (
        sum_scratch[0, :band_rows] + sum_scratch[1, :band_rows] + sum_scratch[2, :band_rows]
    )
    sig = 1.0 / (1.0 + jnp.exp(-my_tile))
    slope = sig * (1.0 + my_tile * (1.0 - sig))
    my_up = up_scratch[1, :, pl.ds(my_row, band_rows)].astype(F32)
    grad_ref[...] = (my_up + sum_scratch[2:, :band_rows] * slope).astype(BF16)


def unit(length, blocks_mine, blocks_other, cots, scale, share):
    frames, band_rows, columns, channels = cots[0].shape
    rows = 2 * band_rows
    side = len(blocks_mine)
    band = jax.ShapeDtypeStruct(cots[0].shape, BF16)
    part = jax.ShapeDtypeStruct((side, share, channels), BF16)
    flops = 2 * 27 * channels * channels * frames * rows * columns * 4
    outs = pl.pallas_call(
        functools.partial(unit_kernel, scale=scale, side=side, share=share),
        out_shape=[band, band] + [part] * side,
        in_specs=scalars(1) + whole(2 * side + 2),
        out_specs=whole(2 + side),
        scratch_shapes=[
            pltpu.VMEM((2, 27 * channels, channels), F32),
            pltpu.VMEM((2, 3, 9, channels, channels), BF16),
            pltpu.VMEM((2, 3, channels, 9 * channels), BF16),
            pltpu.VMEM((frames, rows, columns, channels), F32),
            pltpu.VMEM((frames, rows, columns, channels), BF16),
            pltpu.VMEM((2, frames + 2, rows, columns, 9 * channels), BF16),
            pltpu.VMEM((frames, rows, columns, 9 * channels), BF16),
            pltpu.VMEM((2, frames, rows, columns, channels), BF16),
            pltpu.VMEM((frames + 2, rows, columns, channels), F32),
        ],
        compiler_params=pltpu.CompilerParams(vmem_limit_bytes=48 * 1024 * 1024),
        cost_estimate=pl.CostEstimate(flops=flops, bytes_accessed=4_000_000, transcendentals=0),
    )(length, *blocks_mine, *blocks_other, *cots)
    return outs[0], outs[1], outs[2:]


def total_of(refs, at):
    total = refs[0][at].astype(F32)
    for ref in refs[1:]:
        total = total + ref[at].astype(F32)
    return total


def middle_kernel(*refs):
    side = len(refs) // 2
    core, high, low = position(side)
    p, _ = walk(core, high, low)
    for k in range(side):
        refs[side + k][...] = total_of(refs[:side], jnp.bitwise_xor(p, k)).astype(BF16)


def middle(parts):
    side = len(parts)
    return pl.pallas_call(
        middle_kernel,
        out_shape=[jax.ShapeDtypeStruct(parts[0].shape[1:], BF16)] * side,
        in_specs=whole(side),
        out_specs=whole(side),
    )(*parts)


def last_kernel(*refs):
    refs[-1][...] = total_of(refs[:-1], ...)


def last(parts):
    return pl.pallas_call(
        last_kernel,
        out_shape=jax.ShapeDtypeStruct(parts[0].shape, F32),
        in_specs=whole(len(parts)),
        out_specs=whole(1)[0],
    )(*parts)


def body_pair(slabs, dest, pos, lengths, cot, w_first, w_second):
    wide_size = lax.axis_size("wide")
    side = math.isqrt(wide_size)
    core = lax.axis_index("rows")
    frames, band_rows, columns, channels = cot.shape[1:]
    share = w_first.shape[0]
    base = padded_rows(share)

    def exchange(block):
        return lax.ppermute(block, "rows", [(0, 1), (1, 0)])

    def pairs(step, k):
        both = []
        for chip in range(wide_size):
            high, low = chip // side, chip % side
            to_high, to_low = (high ^ k) * side + low, high * side + (low ^ k)
            targets = (to_high, to_low) if step == 0 else (to_low, to_high)
            both += [(chip * 2 + c, targets[c] * 2 + c) for c in range(2)]
        return both

    def send(blocks, step):
        sent = [lax.ppermute(blocks[k], ("wide", "rows"), pairs(step, k)) for k in range(1, side)]
        return [blocks[0]] + sent

    packed = pack(dest[0, 0], pos[0, 0], slabs[0, 0], w_first, w_second, side)
    relayed = relay(send(packed, 0), columns, base)
    blocks_mine = send(relayed, 1)
    blocks_other = [exchange(block) for block in blocks_mine]
    cots = (cot[0], exchange(cot[0]))

    scale = 1.0 / math.sqrt(frames * band_rows * columns * 2 * wide_size)
    block_out, grad_input, parts = unit(lengths, blocks_mine, blocks_other, cots, scale, share)

    total = last(send(middle(send(parts, 1)), 0))
    total_other = exchange(total)
    share_first = jnp.where(core == 0, total, total_other)
    share_second = jnp.where(core == 0, total_other, total)
    return (block_out[None], grad_input[None], share_first, share_second)


def solution(mesh):
    side = math.isqrt(mesh.shape["wide"])
    square = side * side == mesh.shape["wide"] and side & (side - 1) == 0
    body = body_pair if mesh.shape["rows"] == 2 and square else body_general
    return jax.shard_map(
        body,
        mesh=mesh,
        in_specs=(
            P("wide", "rows", None, None, None),
            P("wide", "rows", None),
            P("wide", "rows", None),
            P("wide"),
            P("wide", None, "rows", None, None),
            P("wide", None),
            P("wide", None),
        ),
        out_specs=(
            P("wide", None, "rows", None, None),
            P("wide", None, "rows", None, None),
            P("wide", None),
            P("wide", None),
        ),
        check_vma=False,
    )
```

```python
import functools
import math

import jax
import jax.numpy as jnp
from jax import lax
from jax.experimental import pallas as pl
from jax.experimental.pallas import tpu as pltpu
from jax.sharding import PartitionSpec as P

BF16 = jnp.bfloat16
F32 = jnp.float32
LABEL_ROWS = 16
SMALL = pltpu.CompilerParams(vmem_limit_bytes=8 * 1024 * 1024)


def with_halo(block, sides, width):
    for axis, dim in sides:
        count = lax.axis_size(axis)
        forward = [(i, i + 1) for i in range(count - 1)]
        backward = [(target, source) for source, target in forward]
        low = lax.ppermute(
            lax.slice_in_dim(block, block.shape[dim] - width, None, axis=dim), axis, forward
        )
        high = lax.ppermute(lax.slice_in_dim(block, 0, width, axis=dim), axis, backward)
        block = jnp.concatenate([low, block, high], axis=dim)
    return block


def silu_slope(values):
    sig = jax.nn.sigmoid(values)
    return sig * (1.0 + values * (1.0 - sig))


def conv_forward(extended, kernel):
    padded = jnp.concatenate([extended[:1], extended[:1], extended], axis=0)
    result = lax.conv_general_dilated(
        padded[None],
        kernel,
        (1, 1, 1),
        ((0, 0), (0, 0), (1, 1)),
        dimension_numbers=("NDHWC", "DHWIO", "NDHWC"),
        preferred_element_type=jnp.float32,
    )
    return result[0]


def conv_weight_grad(extended, upstream):
    padded = jnp.concatenate([extended[:1], extended[:1], extended], axis=0)
    result = lax.conv_general_dilated(
        padded[None],
        upstream[None],
        (1, 1, 1),
        ((0, 0), (0, 0), (1, 1)),
        dimension_numbers=("CDHWN", "IDHWO", "NDHWC"),
        preferred_element_type=jnp.float32,
    )
    channels = extended.shape[-1]
    return jnp.transpose(result, (1, 2, 3, 0, 4)).reshape(27 * channels, upstream.shape[-1])


def conv_data_grad(upstream_ext, kernel):
    padded = jnp.pad(upstream_ext, ((2, 2), (0, 0), (0, 0), (0, 0)))
    flipped = kernel[::-1, ::-1, ::-1]
    result = lax.conv_general_dilated(
        padded[None],
        flipped,
        (1, 1, 1),
        ((0, 0), (0, 0), (1, 1)),
        dimension_numbers=("NDHWC", "DHWOI", "NDHWC"),
        preferred_element_type=jnp.float32,
    )[0]
    head = (result[0] + result[1] + result[2])[None]
    return jnp.concatenate([head, result[3:]], axis=0)


def body_general(slabs, dest, pos, lengths, cot, w_first, w_second):
    wide_size = lax.axis_size("wide")
    band_count = lax.axis_size("rows")
    slab_count = slabs.shape[2]
    columns = slabs.shape[3]
    channels = slabs.shape[4]
    frames = cot.shape[1]
    band_rows = cot.shape[2]
    capacity = -(-slab_count // wide_size)
    slot_count = wide_size * capacity
    targets = dest[0, 0]
    places = pos[0, 0]
    ranking = jnp.arange(slab_count, dtype=jnp.int32)
    earlier = (targets[None, :] == targets[:, None]) & (ranking[None, :] < ranking[:, None])
    slab_rank = jnp.sum(earlier.astype(jnp.int32), axis=1)
    slot_of = targets * capacity + slab_rank
    placing = slot_of[None, :] == jnp.arange(slot_count, dtype=jnp.int32)[:, None]
    flat_slabs = slabs[0, 0].reshape(slab_count, columns * channels)
    outgoing = jnp.dot(placing.astype(jnp.bfloat16), flat_slabs, preferred_element_type=jnp.float32)
    outgoing = outgoing.astype(jnp.bfloat16).reshape(wide_size, capacity, columns * channels)
    labels = jnp.sum(jnp.where(placing, places[None, :] + 1, 0), axis=1) - 1
    labels = labels.reshape(wide_size, capacity)
    arrived, arrived_places = (
        lax.all_to_all(outgoing, "wide", split_axis=0, concat_axis=0, tiled=True),
        lax.all_to_all(labels, "wide", split_axis=0, concat_axis=0, tiled=True),
    )
    settle = (
        arrived_places.reshape(slot_count)[None, :]
        == jnp.arange(slab_count, dtype=jnp.int32)[:, None]
    )
    tile = jnp.dot(
        settle.astype(jnp.bfloat16),
        arrived.reshape(slot_count, columns * channels),
        preferred_element_type=jnp.float32,
    )
    tile = tile.astype(jnp.bfloat16).reshape(frames, band_rows, columns, channels)
    full_first, full_second = (
        lax.all_gather(w_first, "wide", axis=0, tiled=True),
        lax.all_gather(w_second, "wide", axis=0, tiled=True),
    )
    kernel_first = full_first.reshape(3, 3, 3, channels, channels)
    kernel_second = full_second.reshape(3, 3, 3, channels, channels)
    tile_wide = tile.astype(jnp.float32)
    first = jax.nn.silu(tile_wide).astype(jnp.bfloat16)
    first_ext = with_halo(first, (("rows", 1),), 1)
    act = conv_forward(first_ext, kernel_first).astype(jnp.bfloat16)
    second = jax.nn.silu(act.astype(jnp.float32)).astype(jnp.bfloat16)
    second_ext = with_halo(second, (("rows", 1),), 1)
    block_out = (tile_wide + conv_forward(second_ext, kernel_second)).astype(jnp.bfloat16)
    live = (jnp.arange(frames, dtype=jnp.int32) < lengths[0])[:, None, None, None]
    out_grad = jnp.where(live, cot[0], jnp.zeros_like(cot[0]))
    out_grad_ext = with_halo(out_grad, (("rows", 1),), 1)
    weight_second = conv_weight_grad(second_ext, out_grad)
    hidden_grad = conv_data_grad(out_grad_ext, kernel_second)
    act_grad = (hidden_grad * silu_slope(act.astype(jnp.float32))).astype(jnp.bfloat16)
    act_grad_ext = with_halo(act_grad, (("rows", 1),), 1)
    weight_first = conv_weight_grad(first_ext, act_grad)
    first_grad = conv_data_grad(act_grad_ext, kernel_first)
    grad_input = (out_grad.astype(jnp.float32) + first_grad * silu_slope(tile_wide)).astype(
        jnp.bfloat16
    )
    scale = 1.0 / math.sqrt(frames * band_rows * columns * band_count * wide_size)
    weight_first = weight_first * scale
    weight_second = weight_second * scale
    total_first, total_second = (
        lax.psum(weight_first.astype(jnp.bfloat16), "rows").astype(jnp.float32),
        lax.psum(weight_second.astype(jnp.bfloat16), "rows").astype(jnp.float32),
    )
    share_first, share_second = (
        lax.psum_scatter(total_first, "wide", scatter_dimension=0, tiled=True),
        lax.psum_scatter(total_second, "wide", scatter_dimension=0, tiled=True),
    )
    return (block_out[None], grad_input[None], share_first, share_second)


def whole(count):
    return [pl.BlockSpec(memory_space=pltpu.VMEM)] * count


def scalars(count):
    return [pl.BlockSpec(memory_space=pltpu.SMEM)] * count


def position(side):
    core = lax.axis_index("rows")
    wide = lax.axis_index("wide")
    high, low = wide // side, lax.rem(wide, side)
    return core, high, low


def walk(core, high, low):
    return jnp.where(core == 0, high, low), jnp.where(core == 0, low, high)


def chip_of(core, p, q, side):
    high, low = walk(core, p, q)
    return high * side + low


def padded_rows(rows):
    return -(-rows // 16) * 16


def pack_kernel(dest_ref, pos_ref, slabs_hbm, first_hbm, second_hbm, *refs):
    side = len(refs) - 3
    out_refs = refs[:side]
    slabs_ref, own_ref, sem = refs[side:]
    core, high, low = position(side)
    p, _ = walk(core, high, low)
    count, columns, channels = slabs_ref.shape
    share = own_ref.shape[0]
    base = padded_rows(share)
    load_slabs = pltpu.make_async_copy(slabs_hbm, slabs_ref, sem.at[0])
    load_first = pltpu.make_async_copy(first_hbm, own_ref, sem.at[1])
    load_second = pltpu.make_async_copy(second_hbm, own_ref, sem.at[1])
    load_slabs.start()

    @pl.when(core == 0)
    def _():
        load_first.start()

    @pl.when(core != 0)
    def _():
        load_second.start()

    row = lax.broadcasted_iota(jnp.int32, (LABEL_ROWS, channels), 0)
    load_slabs.wait()
    slabs = [slabs_ref[s].astype(F32) for s in range(count)]
    for k in range(side):
        labels = jnp.full((LABEL_ROWS, channels), -1.0, F32)
        for q in range(side):
            target = chip_of(core, jnp.bitwise_xor(p, k), q, side)
            total = jnp.zeros((columns, channels), F32)
            place = jnp.int32(-1)
            for s in range(count):
                match = dest_ref[s] == target
                total = jnp.where(match, slabs[s], total)
                place = jnp.where(match, pos_ref[s], place)
            labels = jnp.where(row == q, place.astype(F32), labels)
            at = base + q * columns
            out_refs[k][at : at + columns, :] = total.astype(BF16)
        out_refs[k][base + side * columns :, :] = labels.astype(BF16)
    load_first.wait()
    own = own_ref[...].astype(F32)
    own = jnp.concatenate([own, jnp.zeros((base - share, channels), F32)], axis=0).astype(BF16)
    for k in range(side):
        out_refs[k][:base, :] = own


def pack(dest, pos, slabs, first, second, side):
    count, columns, channels = slabs.shape
    rows = padded_rows(first.shape[0]) + side * columns + LABEL_ROWS
    return pl.pallas_call(
        pack_kernel,
        out_shape=[jax.ShapeDtypeStruct((rows, channels), BF16)] * side,
        in_specs=scalars(2) + [pl.BlockSpec(memory_space=pltpu.HBM)] * 3,
        out_specs=whole(side),
        scratch_shapes=[
            pltpu.VMEM(slabs.shape, BF16),
            pltpu.VMEM(first.shape, BF16),
            pltpu.SemaphoreType.DMA((2,)),
        ],
    )(dest, pos, slabs, first, second)


def keep_kernel(in_ref, out_ref):
    out_ref[...] = in_ref[...]


def keep(block):
    return pl.pallas_call(
        keep_kernel,
        out_shape=jax.ShapeDtypeStruct(block.shape, block.dtype),
        in_specs=whole(1),
        out_specs=whole(1)[0],
        compiler_params=SMALL,
    )(block)


def relay_kernel(cot_ref, *refs, columns, base):
    side = len(refs) // 2
    ins, outs = refs[:side][::-1], refs[side:]
    core, high, low = position(side)
    _, q = walk(core, high, low)
    channels = ins[0].shape[1]
    end = side * (base + columns) + LABEL_ROWS
    row = lax.broadcasted_iota(jnp.int32, (LABEL_ROWS, channels), 0)
    for j in range(side):
        target = jnp.bitwise_xor(q, j)
        start = pl.multiple_of(base + target * columns, 16)
        labels = jnp.full((LABEL_ROWS, channels), -1.0, F32)
        for k in range(side):
            outs[j][k * base : (k + 1) * base, :] = ins[k][:base, :]
            at = side * base + k * columns
            outs[j][at : at + columns, :] = ins[k][pl.ds(start, columns), :]
            theirs = ins[k][base + side * columns :, :].astype(F32)
            label = jnp.sum(jnp.where(row == target, theirs, 0.0), axis=0, keepdims=True)
            labels = jnp.where(row == k, label, labels)
        outs[j][end - LABEL_ROWS : end, :] = labels.astype(BF16)
    outs[0][end:, :] = cot_ref[...].reshape(-1, channels)


def relay(cot, ins, columns, base):
    side = len(ins)
    channels = ins[0].shape[1]
    rows = side * (base + columns) + LABEL_ROWS
    extra = cot.size // channels
    return pl.pallas_call(
        functools.partial(relay_kernel, columns=columns, base=base),
        out_shape=[jax.ShapeDtypeStruct((rows + extra, channels), BF16)]
        + [jax.ShapeDtypeStruct((rows, channels), BF16)] * (side - 1),
        in_specs=whole(side + 1),
        out_specs=whole(side),
        compiler_params=SMALL,
    )(cot, *ins[::-1])


def settle(blocks, tile_ref, first_row, base):
    side = len(blocks)
    frames, _, columns, channels = tile_ref.shape
    slots = []
    for block in blocks:
        end = side * (base + columns)
        labels = block[end : end + LABEL_ROWS, :].astype(F32)
        for k in range(side):
            at = side * base + k * columns
            values = block[at : at + columns, :].astype(F32)
            slots.append((labels[k : k + 1], values))
    for place in range(frames * 2):
        total = jnp.zeros((columns, channels), F32)
        for label, values in slots:
            total = total + jnp.where(label == float(place), values, 0.0)
        tile_ref[place // 2, first_row + place % 2] = total


def gather_weight(blocks, wide_ref, core, high, low, share, base):
    side = len(blocks)
    p, q = walk(core, high, low)
    for j in range(side):
        for k in range(side):
            owner = chip_of(core, jnp.bitwise_xor(p, k), jnp.bitwise_xor(q, j), side)
            start = pl.multiple_of(owner * share, 8)
            values = blocks[j][k * base : (k + 1) * base, :].astype(F32)
            wide_ref[core, pl.ds(start, share), :] = values[:share]


def shifted(field):
    shape = field.shape
    column = lax.broadcasted_iota(jnp.int32, shape, len(shape) - 2)
    count = shape[-2]
    flat = field.reshape(-1, shape[-1])
    low = pltpu.roll(flat, 1, 0).reshape(shape)
    high = pltpu.roll(flat, flat.shape[0] - 1, 0).reshape(shape)
    low = jnp.where(column == 0, 0.0, low)
    high = jnp.where(column == count - 1, 0.0, high)
    return low.astype(BF16), field.astype(BF16), high.astype(BF16)


def spread(field, store, flip):
    rows = field.shape[1]
    columns = shifted(field)
    for b in range(3):
        for e in range(3):
            source = columns[2 - e] if flip else columns[e]
            offset = (1 - b) if flip else (b - 1)
            low = max(0, -offset)
            high = min(rows, rows - offset)
            piece = b * 3 + e
            store(low, high, piece, source[:, low + offset : high + offset])
            for row in range(rows):
                if not low <= row < high:
                    store(row, row + 1, piece, jnp.zeros_like(source[:, :1]))


def store_columns(scratch, index, frames, channels):
    def store(low, high, piece, values):
        lanes = slice(piece * channels, (piece + 1) * channels)
        scratch[index, 2:, low:high, :, lanes] = values
        scratch[index, 0, low:high, :, lanes] = values[0]
        scratch[index, 1, low:high, :, lanes] = values[0]

    return store


def store_plain(scratch, channels):
    def store(low, high, piece, values):
        scratch[:, low:high, :, piece * channels : (piece + 1) * channels] = values

    return store


def data_grad(columns, wl_ref, sum_ref):
    frames, rows, count, nine = columns.shape
    channels = wl_ref.shape[1]
    nt = (((1,), (1,)), ((), ()))
    flat = columns.reshape(frames * rows * count, nine)
    sum_ref[...] = jnp.zeros(sum_ref.shape, F32)
    for a in range(3):
        part = lax.dot_general(flat, wl_ref[a], nt, preferred_element_type=F32)
        sum_ref[a : a + frames] += part.reshape(frames, rows, count, channels)
    sum_ref[2] = sum_ref[0] + sum_ref[1] + sum_ref[2]


def act_gradient(out_grad, act, wl_ref, g_ref, sum_ref):
    spread(out_grad.astype(F32), store_plain(g_ref, out_grad.shape[-1]), True)
    data_grad(g_ref[...], wl_ref, sum_ref)
    act = act.astype(F32)
    sig = 1.0 / (1.0 + jnp.exp(-act))
    return (sum_ref[2:] * (sig * (1.0 + act * (1.0 - sig)))).astype(BF16)


def unit_kernel(length_ref, *refs, scale, side, share):
    refs = list(refs)

    def take(count):
        taken = refs[:count]
        del refs[:count]
        return taken

    blocks_mine, blocks_other = take(side), take(side)
    tile_ref, act_scratch, out_grad_ref, act_grad_ref = take(4)
    w_second_ref, wl_first_ref, wl_second_ref = take(3)
    outs = take(side)
    (
        wide_ref,
        w_first_ref,
        x_scratch,
        g_scratch,
        up_scratch,
        sum_scratch,
    ) = refs
    core, high, low = position(side)
    length = length_ref[0]
    frames, rows, columns, channels = tile_ref.shape
    band_rows = rows // 2
    cells = frames * rows * columns
    nine = 9 * channels
    my_row = core * band_rows
    other_row = (1 - core) * band_rows
    base = padded_rows(share)

    settle(blocks_mine, tile_ref, my_row, base)
    settle(blocks_other, tile_ref, other_row, base)
    gather_weight(blocks_mine, wide_ref, core, high, low, share, base)
    gather_weight(blocks_other, wide_ref, 1 - core, high, low, share, base)
    for a in range(3):
        for piece in range(9):
            at = (a * 9 + piece) * channels
            lanes = slice(piece * channels, (piece + 1) * channels)
            values = wide_ref[0, at : at + channels, :].astype(BF16)
            w_first_ref[a, piece] = values
            wl_first_ref[a, :, lanes] = values
            values = wide_ref[1, at : at + channels, :].astype(BF16)
            w_second_ref[a, piece] = values
            wl_second_ref[a, :, lanes] = values

    tile = tile_ref[...]
    first = tile / (1.0 + jnp.exp(-tile))
    spread(first, store_columns(x_scratch, 0, frames, channels), False)

    end = side * (base + columns) + LABEL_ROWS
    band = (frames, band_rows, columns, channels)
    for block, row in ((blocks_mine[0], my_row), (blocks_other[0], other_row)):
        cot = block[end:, :].reshape(band)
        for t in range(frames):
            up_scratch[1, t, pl.ds(row, band_rows)] = jnp.where(
                t < length, cot[t].astype(F32), 0.0
            ).astype(BF16)
    out_grad_ref[...] = up_scratch[1]

    act = jnp.zeros((cells, channels), F32)
    for a in range(3):
        act = act + jnp.dot(
            x_scratch[0, a : a + frames].reshape(cells, nine),
            w_first_ref[a].reshape(nine, channels),
            preferred_element_type=F32,
        )
    act = act.astype(BF16).reshape(frames, rows, columns, channels)
    act_scratch[...] = act
    act = act.astype(F32)
    second = act / (1.0 + jnp.exp(-act))
    spread(second, store_columns(x_scratch, 1, frames, channels), False)

    @pl.when(core == 0)
    def _():
        act_grad_ref[...] = act_gradient(
            up_scratch[1], act_scratch[...], wl_second_ref, g_scratch, sum_scratch
        )
        up_scratch[0] = act_grad_ref[...]

    upstream = up_scratch[core].reshape(cells, channels).astype(F32).T.astype(BF16)
    for a in range(3):
        part = jnp.dot(
            upstream,
            x_scratch[core, a : a + frames].reshape(cells, nine),
            preferred_element_type=F32,
        )
        for piece in range(9):
            at = (a * 9 + piece) * channels
            wide_ref[0, at : at + channels, :] = (
                part[:, piece * channels : (piece + 1) * channels].T * scale
            )
    p, q = walk(core, high, low)
    for k in range(side):
        for j in range(side):
            owner = chip_of(core, j, jnp.bitwise_xor(q, k), side)
            start = pl.multiple_of(owner * share, 8)
            outs[k][j] = wide_ref[0, pl.ds(start, share), :].astype(BF16)


def unit(length, blocks_mine, blocks_other, band, scale, share):
    frames, band_rows, columns, channels = band
    rows = 2 * band_rows
    side = len(blocks_mine)
    field = (frames, rows, columns, channels)
    part = jax.ShapeDtypeStruct((side, share, channels), BF16)
    flops = 2 * 27 * channels * channels * frames * rows * columns * 3
    outs = pl.pallas_call(
        functools.partial(unit_kernel, scale=scale, side=side, share=share),
        out_shape=[
            jax.ShapeDtypeStruct(field, F32),
            jax.ShapeDtypeStruct(field, BF16),
            jax.ShapeDtypeStruct(field, BF16),
            jax.ShapeDtypeStruct(field, BF16),
            jax.ShapeDtypeStruct((3, 9, channels, channels), BF16),
            jax.ShapeDtypeStruct((3, channels, 9 * channels), BF16),
            jax.ShapeDtypeStruct((3, channels, 9 * channels), BF16),
        ]
        + [part] * side,
        in_specs=scalars(1) + whole(2 * side),
        out_specs=whole(7 + side),
        scratch_shapes=[
            pltpu.VMEM((2, 27 * channels, channels), F32),
            pltpu.VMEM((3, 9, channels, channels), BF16),
            pltpu.VMEM((2, frames + 2, rows, columns, 9 * channels), BF16),
            pltpu.VMEM((frames, rows, columns, 9 * channels), BF16),
            pltpu.VMEM((2,) + field, BF16),
            pltpu.VMEM((frames + 2, rows, columns, channels), F32),
        ],
        compiler_params=pltpu.CompilerParams(vmem_limit_bytes=36 * 1024 * 1024),
        cost_estimate=pl.CostEstimate(flops=flops, bytes_accessed=4_000_000, transcendentals=0),
    )(length, *blocks_mine, *blocks_other)
    return outs[:7], outs[7:]


def finish_kernel(
    tile_ref,
    act_ref,
    out_grad_ref,
    act_grad_ref,
    w_second_ref,
    wl_first_ref,
    wl_second_ref,
    block_ref,
    grad_ref,
    x_scratch,
    g_scratch,
    up_scratch,
    full_scratch,
    sum_scratch,
):
    frames, band_rows, columns, channels = block_ref.shape
    nine = 9 * channels
    cells = frames * band_rows * columns
    core = lax.axis_index("rows")
    my_row = core * band_rows
    tile = tile_ref[:, pl.ds(my_row, band_rows)]

    act = act_ref[...].astype(F32)
    second = act / (1.0 + jnp.exp(-act))
    spread(second, store_columns(x_scratch, 0, frames, channels), False)
    out = jnp.zeros((cells, channels), F32)
    for a in range(3):
        out = out + jnp.dot(
            x_scratch[0, a : a + frames, pl.ds(my_row, band_rows)].reshape(cells, nine),
            w_second_ref[a].reshape(nine, channels),
            preferred_element_type=F32,
        )
    block_ref[...] = (tile + out.reshape(block_ref.shape)).astype(BF16)

    @pl.when(core == 0)
    def _():
        up_scratch[...] = act_grad_ref[...]

    @pl.when(core != 0)
    def _():
        up_scratch[...] = act_gradient(
            out_grad_ref[...], act_ref[...], wl_second_ref, g_scratch, full_scratch
        )

    spread(up_scratch[...].astype(F32), store_plain(g_scratch, channels), True)
    data_grad(g_scratch[:, pl.ds(my_row, band_rows)], wl_first_ref, sum_scratch)
    sig = 1.0 / (1.0 + jnp.exp(-tile))
    slope = sig * (1.0 + tile * (1.0 - sig))
    upstream = out_grad_ref[:, pl.ds(my_row, band_rows)].astype(F32)
    grad_ref[...] = (upstream + sum_scratch[2:] * slope).astype(BF16)


def finish(kept):
    frames, rows, columns, channels = kept[0].shape
    band = jax.ShapeDtypeStruct((frames, rows // 2, columns, channels), BF16)
    flops = 2 * 27 * channels * channels * frames * rows * columns
    return pl.pallas_call(
        finish_kernel,
        out_shape=[band] * 2,
        in_specs=whole(len(kept)),
        out_specs=whole(2),
        scratch_shapes=[
            pltpu.VMEM((1, frames + 2, rows, columns, 9 * channels), BF16),
            pltpu.VMEM((frames, rows, columns, 9 * channels), BF16),
            pltpu.VMEM((frames, rows, columns, channels), BF16),
            pltpu.VMEM((frames + 2, rows, columns, channels), F32),
            pltpu.VMEM((frames + 2, rows // 2, columns, channels), F32),
        ],
        compiler_params=pltpu.CompilerParams(vmem_limit_bytes=20 * 1024 * 1024),
        cost_estimate=pl.CostEstimate(flops=flops, bytes_accessed=2_000_000, transcendentals=0),
    )(*kept)


def total_of(refs, at):
    total = refs[0][at].astype(F32)
    for ref in refs[1:]:
        total = total + ref[at].astype(F32)
    return total


def middle_kernel(*refs):
    side = len(refs) // 2
    core, high, low = position(side)
    p, _ = walk(core, high, low)
    for k in range(side):
        refs[side + k][...] = total_of(refs[:side][::-1], jnp.bitwise_xor(p, k)).astype(BF16)


def middle(parts):
    side = len(parts)
    return pl.pallas_call(
        middle_kernel,
        out_shape=[jax.ShapeDtypeStruct(parts[0].shape[1:], BF16)] * side,
        in_specs=whole(side),
        out_specs=whole(side),
        compiler_params=SMALL,
    )(*parts[::-1])


def last_kernel(*refs):
    refs[-1][...] = total_of(refs[:-1][::-1], ...)


def last(parts):
    return pl.pallas_call(
        last_kernel,
        out_shape=jax.ShapeDtypeStruct(parts[0].shape, F32),
        in_specs=whole(len(parts)),
        out_specs=whole(1)[0],
        compiler_params=SMALL,
    )(*parts[::-1])


def body_pair(slabs, dest, pos, lengths, cot, w_first, w_second):
    wide_size = lax.axis_size("wide")
    side = math.isqrt(wide_size)
    core = lax.axis_index("rows")
    frames, band_rows, columns, channels = cot.shape[1:]
    share = w_first.shape[0]
    base = padded_rows(share)

    def exchange(block):
        return lax.ppermute(block, "rows", [(0, 1), (1, 0)])

    def pairs(axes, k):
        both = []
        for chip in range(wide_size):
            high, low = chip // side, chip % side
            targets = ((high ^ k) * side + low, high * side + (low ^ k))
            both += [(chip * 2 + c, targets[axes[c]] * 2 + c) for c in range(2)]
        return both

    def send(blocks, axes):
        sent = [
            lax.ppermute(blocks[k], ("wide", "rows"), pairs(axes, k))
            for k in range(side - 1, 0, -1)
        ]
        return [blocks[0]] + sent[::-1]

    packed = pack(dest[0, 0], pos[0, 0], slabs[0, 0], w_first, w_second, side)
    _, *arrived = send(packed, (0, 1))
    relayed = relay(cot[0], [keep(packed[0]), *arrived], columns, base)
    blocks_mine = send(relayed, (1, 0))
    blocks_other = [exchange(block) for block in blocks_mine]

    scale = 1.0 / math.sqrt(frames * band_rows * columns * 2 * wide_size)
    kept, parts = unit(lengths, blocks_mine, blocks_other, cot.shape[1:], scale, share)
    block_out, grad_input = finish(kept)

    arrived = send(parts, (1, 0))
    *arrived, block_out, grad_input = lax.optimization_barrier((*arrived, block_out, grad_input))
    total = last(send(middle(arrived), (0, 1)))
    total_other = exchange(total)
    share_first = jnp.where(core == 0, total, total_other)
    share_second = jnp.where(core == 0, total_other, total)
    return (block_out[None], grad_input[None], share_first, share_second)


def solution(mesh):
    side = math.isqrt(mesh.shape["wide"])
    square = side * side == mesh.shape["wide"] and side & (side - 1) == 0
    body = body_pair if mesh.shape["rows"] == 2 and square else body_general
    return jax.shard_map(
        body,
        mesh=mesh,
        in_specs=(
            P("wide", "rows", None, None, None),
            P("wide", "rows", None),
            P("wide", "rows", None),
            P("wide"),
            P("wide", None, "rows", None, None),
            P("wide", None),
            P("wide", None),
        ),
        out_specs=(
            P("wide", None, "rows", None, None),
            P("wide", None, "rows", None, None),
            P("wide", None),
            P("wide", None),
        ),
        check_vma=False,
    )
```

```python
import functools
import math

import jax
import jax.numpy as jnp
from jax import lax
from jax.experimental import pallas as pl
from jax.experimental.pallas import tpu as pltpu
from jax.sharding import PartitionSpec as P

BF16 = jnp.bfloat16
F32 = jnp.float32
SMALL = pltpu.CompilerParams(vmem_limit_bytes=8 * 1024 * 1024)


def with_halo(block, sides, width):
    for axis, dim in sides:
        count = lax.axis_size(axis)
        forward = [(i, i + 1) for i in range(count - 1)]
        backward = [(target, source) for source, target in forward]
        low = lax.ppermute(
            lax.slice_in_dim(block, block.shape[dim] - width, None, axis=dim), axis, forward
        )
        high = lax.ppermute(lax.slice_in_dim(block, 0, width, axis=dim), axis, backward)
        block = jnp.concatenate([low, block, high], axis=dim)
    return block


def silu_slope(values):
    sig = jax.nn.sigmoid(values)
    return sig * (1.0 + values * (1.0 - sig))


def conv_forward(extended, kernel):
    padded = jnp.concatenate([extended[:1], extended[:1], extended], axis=0)
    result = lax.conv_general_dilated(
        padded[None],
        kernel,
        (1, 1, 1),
        ((0, 0), (0, 0), (1, 1)),
        dimension_numbers=("NDHWC", "DHWIO", "NDHWC"),
        preferred_element_type=jnp.float32,
    )
    return result[0]


def conv_weight_grad(extended, upstream):
    padded = jnp.concatenate([extended[:1], extended[:1], extended], axis=0)
    result = lax.conv_general_dilated(
        padded[None],
        upstream[None],
        (1, 1, 1),
        ((0, 0), (0, 0), (1, 1)),
        dimension_numbers=("CDHWN", "IDHWO", "NDHWC"),
        preferred_element_type=jnp.float32,
    )
    channels = extended.shape[-1]
    return jnp.transpose(result, (1, 2, 3, 0, 4)).reshape(27 * channels, upstream.shape[-1])


def conv_data_grad(upstream_ext, kernel):
    padded = jnp.pad(upstream_ext, ((2, 2), (0, 0), (0, 0), (0, 0)))
    flipped = kernel[::-1, ::-1, ::-1]
    result = lax.conv_general_dilated(
        padded[None],
        flipped,
        (1, 1, 1),
        ((0, 0), (0, 0), (1, 1)),
        dimension_numbers=("NDHWC", "DHWOI", "NDHWC"),
        preferred_element_type=jnp.float32,
    )[0]
    head = (result[0] + result[1] + result[2])[None]
    return jnp.concatenate([head, result[3:]], axis=0)


def body_general(slabs, dest, pos, lengths, cot, w_first, w_second):
    wide_size = lax.axis_size("wide")
    band_count = lax.axis_size("rows")
    slab_count = slabs.shape[2]
    columns = slabs.shape[3]
    channels = slabs.shape[4]
    frames = cot.shape[1]
    band_rows = cot.shape[2]
    capacity = -(-slab_count // wide_size)
    slot_count = wide_size * capacity
    targets = dest[0, 0]
    places = pos[0, 0]
    ranking = jnp.arange(slab_count, dtype=jnp.int32)
    earlier = (targets[None, :] == targets[:, None]) & (ranking[None, :] < ranking[:, None])
    slab_rank = jnp.sum(earlier.astype(jnp.int32), axis=1)
    slot_of = targets * capacity + slab_rank
    placing = slot_of[None, :] == jnp.arange(slot_count, dtype=jnp.int32)[:, None]
    flat_slabs = slabs[0, 0].reshape(slab_count, columns * channels)
    outgoing = jnp.dot(placing.astype(jnp.bfloat16), flat_slabs, preferred_element_type=jnp.float32)
    outgoing = outgoing.astype(jnp.bfloat16).reshape(wide_size, capacity, columns * channels)
    labels = jnp.sum(jnp.where(placing, places[None, :] + 1, 0), axis=1) - 1
    labels = labels.reshape(wide_size, capacity)
    arrived, arrived_places = (
        lax.all_to_all(outgoing, "wide", split_axis=0, concat_axis=0, tiled=True),
        lax.all_to_all(labels, "wide", split_axis=0, concat_axis=0, tiled=True),
    )
    settle = (
        arrived_places.reshape(slot_count)[None, :]
        == jnp.arange(slab_count, dtype=jnp.int32)[:, None]
    )
    tile = jnp.dot(
        settle.astype(jnp.bfloat16),
        arrived.reshape(slot_count, columns * channels),
        preferred_element_type=jnp.float32,
    )
    tile = tile.astype(jnp.bfloat16).reshape(frames, band_rows, columns, channels)
    full_first, full_second = (
        lax.all_gather(w_first, "wide", axis=0, tiled=True),
        lax.all_gather(w_second, "wide", axis=0, tiled=True),
    )
    kernel_first = full_first.reshape(3, 3, 3, channels, channels)
    kernel_second = full_second.reshape(3, 3, 3, channels, channels)
    tile_wide = tile.astype(jnp.float32)
    first = jax.nn.silu(tile_wide).astype(jnp.bfloat16)
    first_ext = with_halo(first, (("rows", 1),), 1)
    act = conv_forward(first_ext, kernel_first).astype(jnp.bfloat16)
    second = jax.nn.silu(act.astype(jnp.float32)).astype(jnp.bfloat16)
    second_ext = with_halo(second, (("rows", 1),), 1)
    block_out = (tile_wide + conv_forward(second_ext, kernel_second)).astype(jnp.bfloat16)
    live = (jnp.arange(frames, dtype=jnp.int32) < lengths[0])[:, None, None, None]
    out_grad = jnp.where(live, cot[0], jnp.zeros_like(cot[0]))
    out_grad_ext = with_halo(out_grad, (("rows", 1),), 1)
    weight_second = conv_weight_grad(second_ext, out_grad)
    hidden_grad = conv_data_grad(out_grad_ext, kernel_second)
    act_grad = (hidden_grad * silu_slope(act.astype(jnp.float32))).astype(jnp.bfloat16)
    act_grad_ext = with_halo(act_grad, (("rows", 1),), 1)
    weight_first = conv_weight_grad(first_ext, act_grad)
    first_grad = conv_data_grad(act_grad_ext, kernel_first)
    grad_input = (out_grad.astype(jnp.float32) + first_grad * silu_slope(tile_wide)).astype(
        jnp.bfloat16
    )
    scale = 1.0 / math.sqrt(frames * band_rows * columns * band_count * wide_size)
    weight_first = weight_first * scale
    weight_second = weight_second * scale
    total_first, total_second = (
        lax.psum(weight_first.astype(jnp.bfloat16), "rows").astype(jnp.float32),
        lax.psum(weight_second.astype(jnp.bfloat16), "rows").astype(jnp.float32),
    )
    share_first, share_second = (
        lax.psum_scatter(total_first, "wide", scatter_dimension=0, tiled=True),
        lax.psum_scatter(total_second, "wide", scatter_dimension=0, tiled=True),
    )
    return (block_out[None], grad_input[None], share_first, share_second)


def whole(count):
    return [pl.BlockSpec(memory_space=pltpu.VMEM)] * count


def scalars(count):
    return [pl.BlockSpec(memory_space=pltpu.SMEM)] * count


def position(side):
    core = lax.axis_index("rows")
    wide = lax.axis_index("wide")
    high, low = wide // side, lax.rem(wide, side)
    return core, high, low


def walk(core, high, low):
    return jnp.where(core == 0, high, low), jnp.where(core == 0, low, high)


def chip_of(core, p, q, side):
    high, low = walk(core, p, q)
    return high * side + low


def block_rows(share):
    return -(-(share + 8) // 16) * 16


def pack_kernel(dest_ref, pos_ref, slabs_hbm, first_hbm, second_hbm, *refs):
    side = len(refs) - 4
    out_refs = refs[:side]
    slabs_ref, own_ref, block_ref, sem = refs[side:]
    core, high, low = position(side)
    p, _ = walk(core, high, low)
    count, columns, channels = slabs_ref.shape
    share = own_ref.shape[0]
    base = block_rows(share)
    load_slabs = pltpu.make_async_copy(slabs_hbm, slabs_ref, sem.at[0])
    load_first = pltpu.make_async_copy(first_hbm, own_ref, sem.at[1])
    load_second = pltpu.make_async_copy(second_hbm, own_ref, sem.at[1])
    load_slabs.start()

    @pl.when(core == 0)
    def _():
        load_first.start()

    @pl.when(core != 0)
    def _():
        load_second.start()

    block_ref[...] = jnp.zeros(block_ref.shape, BF16)
    row = lax.broadcasted_iota(jnp.int32, (base - share, channels), 0)
    labels = [jnp.full((base - share, channels), -1.0, F32) for _ in range(side)]
    steps, slots = [], []
    for s in range(count):
        p_to, q_to = walk(core, dest_ref[s] // side, lax.rem(dest_ref[s], side))
        steps.append(jnp.bitwise_xor(p, p_to))
        slots.append(q_to)
        place = pos_ref[s].astype(F32)
        for k in range(side):
            hit = jnp.where(steps[s] == k, q_to, -1)
            labels[k] = jnp.where(row == hit, place, labels[k])
    load_slabs.wait()
    for s in range(count):
        start = pl.multiple_of(slots[s] * columns, columns)
        block_ref[steps[s], pl.ds(start, columns), :] = slabs_ref[s]
    for k in range(side):
        out_refs[k][base:, :] = block_ref[k]
    load_first.wait()
    own = own_ref[...].astype(F32)
    for k in range(side):
        out_refs[k][:base, :] = jnp.concatenate([own, labels[k]], axis=0).astype(BF16)


def pack(dest, pos, slabs, first, second, side):
    count, columns, channels = slabs.shape
    rows = block_rows(first.shape[0]) + side * columns
    return pl.pallas_call(
        pack_kernel,
        out_shape=[jax.ShapeDtypeStruct((rows, channels), BF16)] * side,
        in_specs=scalars(2) + [pl.BlockSpec(memory_space=pltpu.HBM)] * 3,
        out_specs=whole(side),
        scratch_shapes=[
            pltpu.VMEM(slabs.shape, BF16),
            pltpu.VMEM(first.shape, BF16),
            pltpu.VMEM((side, side * columns, channels), BF16),
            pltpu.SemaphoreType.DMA((2,)),
        ],
    )(dest, pos, slabs, first, second)


def keep_kernel(*refs):
    half = len(refs) // 2
    for source, target in zip(refs[:half], refs[half:]):
        target[...] = source[...]


def keep(*blocks):
    return pl.pallas_call(
        keep_kernel,
        out_shape=[jax.ShapeDtypeStruct(block.shape, block.dtype) for block in blocks],
        in_specs=whole(len(blocks)),
        out_specs=whole(len(blocks)),
        compiler_params=SMALL,
    )(*blocks)


def relay_kernel(cot_ref, *refs, columns, base):
    side = len(refs) // 2
    ins, outs = refs[:side][::-1], refs[side:]
    core, high, low = position(side)
    _, q = walk(core, high, low)
    for j in range(side):
        start = pl.multiple_of(base + jnp.bitwise_xor(q, j) * columns, 16)
        for k in range(side):
            outs[j][k * base : (k + 1) * base, :] = ins[k][:base, :]
            at = side * base + k * columns
            outs[j][at : at + columns, :] = ins[k][pl.ds(start, columns), :]
    outs[0][side * (base + columns) :, :] = cot_ref[...].reshape(-1, cot_ref.shape[-1])


def relay(cot, ins, columns, base):
    side = len(ins)
    channels = ins[0].shape[1]
    rows = side * (base + columns)
    extra = cot.size // channels
    return pl.pallas_call(
        functools.partial(relay_kernel, columns=columns, base=base),
        out_shape=[jax.ShapeDtypeStruct((rows + extra, channels), BF16)]
        + [jax.ShapeDtypeStruct((rows, channels), BF16)] * (side - 1),
        in_specs=whole(side + 1),
        out_specs=whole(side),
        compiler_params=SMALL,
    )(cot, *ins[::-1])


def settle(blocks, tile_ref, first_row, q, share):
    side = len(blocks)
    base = block_rows(share)
    frames, _, columns, channels = tile_ref.shape
    row = lax.broadcasted_iota(jnp.int32, (base - share, channels), 0)
    slots = []
    for block in blocks:
        for k in range(side):
            labels = block[k * base : (k + 1) * base, :].astype(F32)[share:]
            label = jnp.sum(jnp.where(row == q, labels, 0.0), axis=0, keepdims=True)
            label = jnp.broadcast_to(label, (columns, channels)).astype(BF16)
            at = side * base + k * columns
            slots.append((label, block[at : at + columns, :]))
    for place in range(frames * 2):
        total = jnp.zeros((columns, channels), BF16)
        for label, values in slots:
            total = jnp.where(label == BF16(place), values, total)
        tile_ref[place // 2, first_row + place % 2] = total.astype(F32)


def gather_weight(blocks, wide_ref, core, high, low, share, base):
    side = len(blocks)
    p, q = walk(core, high, low)
    for j in range(side):
        for k in range(side):
            owner = chip_of(core, jnp.bitwise_xor(p, k), jnp.bitwise_xor(q, j), side)
            start = pl.multiple_of(owner * share, 8)
            values = blocks[j][k * base : (k + 1) * base, :].astype(F32)
            wide_ref[core, pl.ds(start, share), :] = values[:share]


def shifted(field):
    shape = field.shape
    column = lax.broadcasted_iota(jnp.int32, shape, len(shape) - 2)
    count = shape[-2]
    flat = field.reshape(-1, shape[-1])
    low = pltpu.roll(flat, 1, 0).reshape(shape)
    high = pltpu.roll(flat, flat.shape[0] - 1, 0).reshape(shape)
    low = jnp.where(column == 0, 0.0, low)
    high = jnp.where(column == count - 1, 0.0, high)
    return low.astype(BF16), field.astype(BF16), high.astype(BF16)


def spread(field, store, flip):
    rows = field.shape[1]
    columns = shifted(field)
    for b in range(3):
        for e in range(3):
            source = columns[2 - e] if flip else columns[e]
            offset = (1 - b) if flip else (b - 1)
            low = max(0, -offset)
            high = min(rows, rows - offset)
            piece = b * 3 + e
            store(low, high, piece, source[:, low + offset : high + offset])
            for row in range(rows):
                if not low <= row < high:
                    store(row, row + 1, piece, jnp.zeros_like(source[:, :1]))


def store_pieces(columns_ref):
    channels = columns_ref.shape[-1] // 9

    def store(low, high, piece, values):
        columns_ref[:, low:high, :, piece * channels : (piece + 1) * channels] = values

    return store


def spread_weight(wide_ref, index, out_ref, transposed):
    channels = wide_ref.shape[-1]
    for a in range(3):
        for piece in range(9):
            at = (a * 9 + piece) * channels
            values = wide_ref[index, at : at + channels, :].astype(BF16)
            frame = slice(a * channels, (a + 1) * channels)
            place = slice(piece * channels, (piece + 1) * channels)
            if transposed:
                out_ref[frame, place] = values
            else:
                out_ref[place, frame] = values


def conv(columns, w_ref, frames):
    channels = w_ref.shape[1] // 3
    product = jnp.dot(columns, w_ref[...], preferred_element_type=F32)
    product = product.reshape(frames, -1, 3 * channels)
    parts = [product[:, :, a * channels : (a + 1) * channels] for a in range(3)]
    out = []
    for t in range(frames):
        out.append(parts[0][max(t - 2, 0)] + parts[1][max(t - 1, 0)] + parts[2][t])
    return out


def conv_back(columns, wl_ref, frames):
    channels = wl_ref.shape[0] // 3
    nt = (((1,), (1,)), ((), ()))
    product = lax.dot_general(columns, wl_ref[...], nt, preferred_element_type=F32)
    product = product.reshape(frames, -1, 3 * channels)
    parts = [product[:, :, a * channels : (a + 1) * channels] for a in range(3)]
    out = []
    for t in range(frames):
        total = parts[2][t]
        for a in range(2):
            for source in range(frames):
                if max(source + a - 2, 0) == t:
                    total = total + parts[a][source]
        out.append(total)
    return out


def act_gradient(out_grad, act, wl_ref, columns_ref, store):
    spread(out_grad.astype(F32), store_pieces(columns_ref), True)
    frames, rows, count, nine = columns_ref.shape
    hidden = conv_back(columns_ref[...].reshape(-1, nine), wl_ref, frames)
    for t in range(frames):
        value = act[t].astype(F32)
        sig = 1.0 / (1.0 + jnp.exp(-value))
        slope = sig * (1.0 + value * (1.0 - sig))
        store(t, (hidden[t].reshape(value.shape) * slope).astype(BF16))


def unit_kernel(length_ref, *refs, scale, side, share):
    refs = list(refs)

    def take(count):
        taken = refs[:count]
        del refs[:count]
        return taken

    blocks_mine, blocks_other = take(side), take(side)
    tile_ref, act_ref, out_grad_ref, act_grad_ref, wide_ref = take(5)
    outs = take(side)
    w_ref, wl_ref, total_ref, x_scratch, g_scratch, left_ref = refs
    core, high, low = position(side)
    length = length_ref[0]
    frames, rows, columns, channels = tile_ref.shape
    band_rows = rows // 2
    cells = frames * rows * columns
    nine = 9 * channels
    my_row = core * band_rows
    other_row = (1 - core) * band_rows
    base = block_rows(share)

    _, my_q = walk(core, high, low)
    _, other_q = walk(1 - core, high, low)
    settle(blocks_mine, tile_ref, my_row, my_q, share)
    settle(blocks_other, tile_ref, other_row, other_q, share)
    gather_weight(blocks_mine, wide_ref, core, high, low, share, base)
    gather_weight(blocks_other, wide_ref, 1 - core, high, low, share, base)
    spread_weight(wide_ref, 0, w_ref, False)

    tile = tile_ref[...]
    first = tile / (1.0 + jnp.exp(-tile))
    spread(first, store_pieces(x_scratch.at[0]), False)

    end = side * (base + columns)
    band = (frames, band_rows, columns, channels)
    for block, row in ((blocks_mine[0], my_row), (blocks_other[0], other_row)):
        cot = block[end:, :].reshape(band)
        for t in range(frames):
            out_grad_ref[t, pl.ds(row, band_rows)] = jnp.where(
                t < length, cot[t].astype(F32), 0.0
            ).astype(BF16)
    act = conv(x_scratch[0].reshape(cells, nine), w_ref, frames)
    for t in range(frames):
        act_ref[t] = act[t].astype(BF16).reshape(rows, columns, channels)
    act = act_ref[...].astype(F32)
    second = act / (1.0 + jnp.exp(-act))
    spread(second, store_pieces(x_scratch.at[1]), False)

    @pl.when(core == 0)
    def _():
        def store(t, values):
            act_grad_ref[t] = values

        spread_weight(wide_ref, 1, wl_ref, True)
        act_gradient(out_grad_ref[...], act_ref, wl_ref, g_scratch, store)

    upstream = jnp.where(core == 0, act_grad_ref[...].astype(F32), out_grad_ref[...].astype(F32))
    upstream = upstream.reshape(frames, rows * columns, channels)
    turned = [upstream[t].T for t in range(frames)]
    for a in range(3):
        for t in range(frames):
            met = [turned[s] for s in range(frames) if max(s + a - 2, 0) == t]
            met = sum(met[1:], met[0]) if met else jnp.zeros_like(turned[0])
            frame = slice(a * channels, (a + 1) * channels)
            left_ref[frame, t * rows * columns : (t + 1) * rows * columns] = met.astype(BF16)
    product = jnp.dot(
        left_ref[...], x_scratch[core].reshape(cells, nine), preferred_element_type=F32
    )
    for a in range(3):
        for piece in range(9):
            at = (a * 9 + piece) * channels
            block = product[a * channels : (a + 1) * channels, piece * channels : (piece + 1) * channels]
            total_ref[at : at + channels, :] = block.T * scale
    p, q = walk(core, high, low)
    for k in range(side):
        for j in range(side):
            owner = chip_of(core, j, jnp.bitwise_xor(q, k), side)
            start = pl.multiple_of(owner * share, 8)
            outs[k][j] = total_ref[pl.ds(start, share), :].astype(BF16)


def unit(length, blocks_mine, blocks_other, band, scale, share):
    frames, band_rows, columns, channels = band
    rows = 2 * band_rows
    side = len(blocks_mine)
    field = (frames, rows, columns, channels)
    cells = frames * rows * columns
    part = jax.ShapeDtypeStruct((side, share, channels), BF16)
    flops = 2 * 27 * channels * channels * cells * 3
    outs = pl.pallas_call(
        functools.partial(unit_kernel, scale=scale, side=side, share=share),
        out_shape=[
            jax.ShapeDtypeStruct(field, F32),
            jax.ShapeDtypeStruct(field, BF16),
            jax.ShapeDtypeStruct(field, BF16),
            jax.ShapeDtypeStruct(field, BF16),
            jax.ShapeDtypeStruct((2, 27 * channels, channels), F32),
        ]
        + [part] * side,
        in_specs=scalars(1) + whole(2 * side),
        out_specs=whole(5 + side),
        scratch_shapes=[
            pltpu.VMEM((9 * channels, 3 * channels), BF16),
            pltpu.VMEM((3 * channels, 9 * channels), BF16),
            pltpu.VMEM((27 * channels, channels), F32),
            pltpu.VMEM((2, frames, rows, columns, 9 * channels), BF16),
            pltpu.VMEM((frames, rows, columns, 9 * channels), BF16),
            pltpu.VMEM((3 * channels, cells), BF16),
        ],
        compiler_params=pltpu.CompilerParams(vmem_limit_bytes=36 * 1024 * 1024),
        cost_estimate=pl.CostEstimate(flops=flops, bytes_accessed=4_000_000, transcendentals=0),
    )(length, *blocks_mine, *blocks_other)
    return outs[:5], outs[5:]


def finish_kernel(
    tile_ref,
    act_ref,
    out_grad_ref,
    act_grad_ref,
    wide_ref,
    block_ref,
    grad_ref,
    w_ref,
    wl_ref,
    columns_ref,
    up_ref,
):
    frames, band_rows, columns, channels = block_ref.shape
    nine = 9 * channels
    core = lax.axis_index("rows")
    my_row = core * band_rows
    mine = pl.ds(my_row, band_rows)
    shape = (band_rows, columns, channels)

    act = act_ref[...].astype(F32)
    second = act / (1.0 + jnp.exp(-act))
    spread(second, store_pieces(columns_ref), False)
    spread_weight(wide_ref, 1, w_ref, False)
    out = conv(columns_ref[:, mine].reshape(-1, nine), w_ref, frames)
    for t in range(frames):
        block_ref[t] = (tile_ref[t, mine] + out[t].reshape(shape)).astype(BF16)

    @pl.when(core == 0)
    def _():
        up_ref[...] = act_grad_ref[...]

    @pl.when(core != 0)
    def _():
        def store(t, values):
            up_ref[t] = values

        spread_weight(wide_ref, 1, wl_ref, True)
        act_gradient(out_grad_ref[...], act_ref, wl_ref, columns_ref, store)

    spread(up_ref[...].astype(F32), store_pieces(columns_ref), True)
    spread_weight(wide_ref, 0, wl_ref, True)
    out = conv_back(columns_ref[:, mine].reshape(-1, nine), wl_ref, frames)
    for t in range(frames):
        tile = tile_ref[t, mine]
        sig = 1.0 / (1.0 + jnp.exp(-tile))
        slope = sig * (1.0 + tile * (1.0 - sig))
        upstream = out_grad_ref[t, mine].astype(F32)
        grad_ref[t] = (upstream + out[t].reshape(shape) * slope).astype(BF16)


def finish(kept):
    frames, rows, columns, channels = kept[0].shape
    band = jax.ShapeDtypeStruct((frames, rows // 2, columns, channels), BF16)
    flops = 2 * 27 * channels * channels * frames * rows * columns
    return pl.pallas_call(
        finish_kernel,
        out_shape=[band] * 2,
        in_specs=whole(len(kept)),
        out_specs=whole(2),
        scratch_shapes=[
            pltpu.VMEM((9 * channels, 3 * channels), BF16),
            pltpu.VMEM((3 * channels, 9 * channels), BF16),
            pltpu.VMEM((frames, rows, columns, 9 * channels), BF16),
            pltpu.VMEM((frames, rows, columns, channels), BF16),
        ],
        compiler_params=pltpu.CompilerParams(vmem_limit_bytes=20 * 1024 * 1024),
        cost_estimate=pl.CostEstimate(flops=flops, bytes_accessed=2_000_000, transcendentals=0),
    )(*kept)


def total_of(refs, at):
    total = refs[0][at].astype(F32)
    for ref in refs[1:]:
        total = total + ref[at].astype(F32)
    return total


def middle_kernel(*refs):
    side = len(refs) // 2
    core, high, low = position(side)
    p, _ = walk(core, high, low)
    for k in range(side):
        refs[side + k][...] = total_of(refs[:side][::-1], jnp.bitwise_xor(p, k)).astype(BF16)


def middle(parts):
    side = len(parts)
    return pl.pallas_call(
        middle_kernel,
        out_shape=[jax.ShapeDtypeStruct(parts[0].shape[1:], BF16)] * side,
        in_specs=whole(side),
        out_specs=whole(side),
        compiler_params=SMALL,
    )(*parts[::-1])


def last_kernel(*refs):
    refs[-1][...] = total_of(refs[:-1][::-1], ...)


def last(parts):
    return pl.pallas_call(
        last_kernel,
        out_shape=jax.ShapeDtypeStruct(parts[0].shape, F32),
        in_specs=whole(len(parts)),
        out_specs=whole(1)[0],
        compiler_params=SMALL,
    )(*parts[::-1])


def body_pair(slabs, dest, pos, lengths, cot, w_first, w_second):
    wide_size = lax.axis_size("wide")
    side = math.isqrt(wide_size)
    core = lax.axis_index("rows")
    frames, band_rows, columns, channels = cot.shape[1:]
    share = w_first.shape[0]
    base = block_rows(share)

    def exchange(block):
        return lax.ppermute(block, "rows", [(0, 1), (1, 0)])

    def pairs(axes, k):
        both = []
        for chip in range(wide_size):
            high, low = chip // side, chip % side
            targets = ((high ^ k) * side + low, high * side + (low ^ k))
            both += [(chip * 2 + c, targets[axes[c]] * 2 + c) for c in range(2)]
        return both

    def send(blocks, axes):
        sent = [
            lax.ppermute(blocks[k], ("wide", "rows"), pairs(axes, k))
            for k in range(side - 1, 0, -1)
        ]
        return [blocks[0]] + sent[::-1]

    packed = pack(dest[0, 0], pos[0, 0], slabs[0, 0], w_first, w_second, side)
    _, *arrived = send(packed, (0, 1))
    kept_block, kept_cot = keep(packed[0], cot[0])
    relayed = relay(kept_cot, [kept_block, *arrived], columns, base)
    blocks_mine = send(relayed, (1, 0))
    blocks_other = [exchange(block) for block in blocks_mine]

    scale = 1.0 / math.sqrt(frames * band_rows * columns * 2 * wide_size)
    kept, parts = unit(lengths, blocks_mine, blocks_other, cot.shape[1:], scale, share)
    block_out, grad_input = finish(kept)

    arrived = send(parts, (1, 0))
    *arrived, block_out, grad_input = lax.optimization_barrier((*arrived, block_out, grad_input))
    total = last(send(middle(arrived), (0, 1)))
    total_other = exchange(total)
    share_first = jnp.where(core == 0, total, total_other)
    share_second = jnp.where(core == 0, total_other, total)
    return (block_out[None], grad_input[None], share_first, share_second)


def solution(mesh):
    side = math.isqrt(mesh.shape["wide"])
    square = side * side == mesh.shape["wide"] and side & (side - 1) == 0
    body = body_pair if mesh.shape["rows"] == 2 and square else body_general
    return jax.shard_map(
        body,
        mesh=mesh,
        in_specs=(
            P("wide", "rows", None, None, None),
            P("wide", "rows", None),
            P("wide", "rows", None),
            P("wide"),
            P("wide", None, "rows", None, None),
            P("wide", None),
            P("wide", None),
        ),
        out_specs=(
            P("wide", None, "rows", None, None),
            P("wide", None, "rows", None, None),
            P("wide", None),
            P("wide", None),
        ),
        check_vma=False,
    )
```

```python
import functools
import math

import jax
import jax.numpy as jnp
from jax import lax
from jax.experimental import pallas as pl
from jax.experimental.pallas import tpu as pltpu
from jax.sharding import PartitionSpec as P

BF16 = jnp.bfloat16
F32 = jnp.float32
SMALL = pltpu.CompilerParams(vmem_limit_bytes=8 * 1024 * 1024)


def with_halo(block, sides, width):
    for axis, dim in sides:
        count = lax.axis_size(axis)
        forward = [(i, i + 1) for i in range(count - 1)]
        backward = [(target, source) for source, target in forward]
        low = lax.ppermute(
            lax.slice_in_dim(block, block.shape[dim] - width, None, axis=dim), axis, forward
        )
        high = lax.ppermute(lax.slice_in_dim(block, 0, width, axis=dim), axis, backward)
        block = jnp.concatenate([low, block, high], axis=dim)
    return block


def silu_slope(values):
    sig = jax.nn.sigmoid(values)
    return sig * (1.0 + values * (1.0 - sig))


def conv_forward(extended, kernel):
    padded = jnp.concatenate([extended[:1], extended[:1], extended], axis=0)
    result = lax.conv_general_dilated(
        padded[None],
        kernel,
        (1, 1, 1),
        ((0, 0), (0, 0), (1, 1)),
        dimension_numbers=("NDHWC", "DHWIO", "NDHWC"),
        preferred_element_type=jnp.float32,
    )
    return result[0]


def conv_weight_grad(extended, upstream):
    padded = jnp.concatenate([extended[:1], extended[:1], extended], axis=0)
    result = lax.conv_general_dilated(
        padded[None],
        upstream[None],
        (1, 1, 1),
        ((0, 0), (0, 0), (1, 1)),
        dimension_numbers=("CDHWN", "IDHWO", "NDHWC"),
        preferred_element_type=jnp.float32,
    )
    channels = extended.shape[-1]
    return jnp.transpose(result, (1, 2, 3, 0, 4)).reshape(27 * channels, upstream.shape[-1])


def conv_data_grad(upstream_ext, kernel):
    padded = jnp.pad(upstream_ext, ((2, 2), (0, 0), (0, 0), (0, 0)))
    flipped = kernel[::-1, ::-1, ::-1]
    result = lax.conv_general_dilated(
        padded[None],
        flipped,
        (1, 1, 1),
        ((0, 0), (0, 0), (1, 1)),
        dimension_numbers=("NDHWC", "DHWOI", "NDHWC"),
        preferred_element_type=jnp.float32,
    )[0]
    head = (result[0] + result[1] + result[2])[None]
    return jnp.concatenate([head, result[3:]], axis=0)


def body_general(slabs, dest, pos, lengths, cot, w_first, w_second):
    wide_size = lax.axis_size("wide")
    band_count = lax.axis_size("rows")
    slab_count = slabs.shape[2]
    columns = slabs.shape[3]
    channels = slabs.shape[4]
    frames = cot.shape[1]
    band_rows = cot.shape[2]
    capacity = -(-slab_count // wide_size)
    slot_count = wide_size * capacity
    targets = dest[0, 0]
    places = pos[0, 0]
    ranking = jnp.arange(slab_count, dtype=jnp.int32)
    earlier = (targets[None, :] == targets[:, None]) & (ranking[None, :] < ranking[:, None])
    slab_rank = jnp.sum(earlier.astype(jnp.int32), axis=1)
    slot_of = targets * capacity + slab_rank
    placing = slot_of[None, :] == jnp.arange(slot_count, dtype=jnp.int32)[:, None]
    flat_slabs = slabs[0, 0].reshape(slab_count, columns * channels)
    outgoing = jnp.dot(placing.astype(jnp.bfloat16), flat_slabs, preferred_element_type=jnp.float32)
    outgoing = outgoing.astype(jnp.bfloat16).reshape(wide_size, capacity, columns * channels)
    labels = jnp.sum(jnp.where(placing, places[None, :] + 1, 0), axis=1) - 1
    labels = labels.reshape(wide_size, capacity)
    arrived, arrived_places = (
        lax.all_to_all(outgoing, "wide", split_axis=0, concat_axis=0, tiled=True),
        lax.all_to_all(labels, "wide", split_axis=0, concat_axis=0, tiled=True),
    )
    settle = (
        arrived_places.reshape(slot_count)[None, :]
        == jnp.arange(slab_count, dtype=jnp.int32)[:, None]
    )
    tile = jnp.dot(
        settle.astype(jnp.bfloat16),
        arrived.reshape(slot_count, columns * channels),
        preferred_element_type=jnp.float32,
    )
    tile = tile.astype(jnp.bfloat16).reshape(frames, band_rows, columns, channels)
    full_first, full_second = (
        lax.all_gather(w_first, "wide", axis=0, tiled=True),
        lax.all_gather(w_second, "wide", axis=0, tiled=True),
    )
    kernel_first = full_first.reshape(3, 3, 3, channels, channels)
    kernel_second = full_second.reshape(3, 3, 3, channels, channels)
    tile_wide = tile.astype(jnp.float32)
    first = jax.nn.silu(tile_wide).astype(jnp.bfloat16)
    first_ext = with_halo(first, (("rows", 1),), 1)
    act = conv_forward(first_ext, kernel_first).astype(jnp.bfloat16)
    second = jax.nn.silu(act.astype(jnp.float32)).astype(jnp.bfloat16)
    second_ext = with_halo(second, (("rows", 1),), 1)
    block_out = (tile_wide + conv_forward(second_ext, kernel_second)).astype(jnp.bfloat16)
    live = (jnp.arange(frames, dtype=jnp.int32) < lengths[0])[:, None, None, None]
    out_grad = jnp.where(live, cot[0], jnp.zeros_like(cot[0]))
    out_grad_ext = with_halo(out_grad, (("rows", 1),), 1)
    weight_second = conv_weight_grad(second_ext, out_grad)
    hidden_grad = conv_data_grad(out_grad_ext, kernel_second)
    act_grad = (hidden_grad * silu_slope(act.astype(jnp.float32))).astype(jnp.bfloat16)
    act_grad_ext = with_halo(act_grad, (("rows", 1),), 1)
    weight_first = conv_weight_grad(first_ext, act_grad)
    first_grad = conv_data_grad(act_grad_ext, kernel_first)
    grad_input = (out_grad.astype(jnp.float32) + first_grad * silu_slope(tile_wide)).astype(
        jnp.bfloat16
    )
    scale = 1.0 / math.sqrt(frames * band_rows * columns * band_count * wide_size)
    weight_first = weight_first * scale
    weight_second = weight_second * scale
    total_first, total_second = (
        lax.psum(weight_first.astype(jnp.bfloat16), "rows").astype(jnp.float32),
        lax.psum(weight_second.astype(jnp.bfloat16), "rows").astype(jnp.float32),
    )
    share_first, share_second = (
        lax.psum_scatter(total_first, "wide", scatter_dimension=0, tiled=True),
        lax.psum_scatter(total_second, "wide", scatter_dimension=0, tiled=True),
    )
    return (block_out[None], grad_input[None], share_first, share_second)


def whole(count):
    return [pl.BlockSpec(memory_space=pltpu.VMEM)] * count


def scalars(count):
    return [pl.BlockSpec(memory_space=pltpu.SMEM)] * count


def position(side):
    core = lax.axis_index("rows")
    wide = lax.axis_index("wide")
    high, low = wide // side, lax.rem(wide, side)
    return core, high, low


def walk(core, high, low):
    return jnp.where(core == 0, high, low), jnp.where(core == 0, low, high)


def chip_of(core, p, q, side):
    high, low = walk(core, p, q)
    return high * side + low


def block_rows(share):
    return -(-(share + 8) // 16) * 16


def pack_kernel(dest_ref, pos_ref, slabs_hbm, first_hbm, second_hbm, *refs):
    side = len(refs) - 4
    out_refs = refs[:side]
    slabs_ref, own_ref, block_ref, sem = refs[side:]
    core, high, low = position(side)
    p, _ = walk(core, high, low)
    count, columns, channels = slabs_ref.shape
    share = own_ref.shape[0]
    base = block_rows(share)
    load_slabs = pltpu.make_async_copy(slabs_hbm, slabs_ref, sem.at[0])
    load_first = pltpu.make_async_copy(first_hbm, own_ref, sem.at[1])
    load_second = pltpu.make_async_copy(second_hbm, own_ref, sem.at[1])
    load_slabs.start()

    @pl.when(core == 0)
    def _():
        load_first.start()

    @pl.when(core != 0)
    def _():
        load_second.start()

    block_ref[...] = jnp.zeros(block_ref.shape, BF16)
    row = lax.broadcasted_iota(jnp.int32, (base - share, channels), 0)
    labels = [jnp.full((base - share, channels), -1.0, F32) for _ in range(side)]
    steps, slots = [], []
    for s in range(count):
        p_to, q_to = walk(core, dest_ref[s] // side, lax.rem(dest_ref[s], side))
        steps.append(jnp.bitwise_xor(p, p_to))
        slots.append(q_to)
        place = pos_ref[s].astype(F32)
        for k in range(side):
            hit = jnp.where(steps[s] == k, q_to, -1)
            labels[k] = jnp.where(row == hit, place, labels[k])
    load_slabs.wait()
    for s in range(count):
        start = pl.multiple_of(slots[s] * columns, columns)
        block_ref[steps[s], pl.ds(start, columns), :] = slabs_ref[s]
    for k in range(side):
        out_refs[k][base:, :] = block_ref[k]
    load_first.wait()
    own = own_ref[...].astype(F32)
    for k in range(side):
        out_refs[k][:base, :] = jnp.concatenate([own, labels[k]], axis=0).astype(BF16)


def pack(dest, pos, slabs, first, second, side):
    count, columns, channels = slabs.shape
    rows = block_rows(first.shape[0]) + side * columns
    return pl.pallas_call(
        pack_kernel,
        out_shape=[jax.ShapeDtypeStruct((rows, channels), BF16)] * side,
        in_specs=scalars(2) + [pl.BlockSpec(memory_space=pltpu.HBM)] * 3,
        out_specs=whole(side),
        scratch_shapes=[
            pltpu.VMEM(slabs.shape, BF16),
            pltpu.VMEM(first.shape, BF16),
            pltpu.VMEM((side, side * columns, channels), BF16),
            pltpu.SemaphoreType.DMA((2,)),
        ],
    )(dest, pos, slabs, first, second)


def keep_kernel(*refs):
    half = len(refs) // 2
    for source, target in zip(refs[:half], refs[half:]):
        target[...] = source[...]


def keep(*blocks):
    return pl.pallas_call(
        keep_kernel,
        out_shape=[jax.ShapeDtypeStruct(block.shape, block.dtype) for block in blocks],
        in_specs=whole(len(blocks)),
        out_specs=whole(len(blocks)),
        compiler_params=SMALL,
    )(*blocks)


def relay_kernel(cot_ref, *refs, columns, base):
    side = len(refs) // 2
    ins, outs = refs[:side][::-1], refs[side:]
    core, high, low = position(side)
    _, q = walk(core, high, low)
    for j in range(side):
        start = pl.multiple_of(base + jnp.bitwise_xor(q, j) * columns, 16)
        for k in range(side):
            outs[j][k * base : (k + 1) * base, :] = ins[k][:base, :]
            at = side * base + k * columns
            outs[j][at : at + columns, :] = ins[k][pl.ds(start, columns), :]
    outs[0][side * (base + columns) :, :] = cot_ref[...].reshape(-1, cot_ref.shape[-1])


def relay(cot, ins, columns, base):
    side = len(ins)
    channels = ins[0].shape[1]
    rows = side * (base + columns)
    extra = cot.size // channels
    return pl.pallas_call(
        functools.partial(relay_kernel, columns=columns, base=base),
        out_shape=[jax.ShapeDtypeStruct((rows + extra, channels), BF16)]
        + [jax.ShapeDtypeStruct((rows, channels), BF16)] * (side - 1),
        in_specs=whole(side + 1),
        out_specs=whole(side),
        compiler_params=SMALL,
    )(cot, *ins[::-1])


def settle(blocks, tile_ref, first_row, q, share):
    side = len(blocks)
    base = block_rows(share)
    frames, _, columns, channels = tile_ref.shape
    row = lax.broadcasted_iota(jnp.int32, (base - share, channels), 0)
    slots = []
    for block in blocks:
        for k in range(side):
            labels = block[k * base : (k + 1) * base, :].astype(F32)[share:]
            label = jnp.sum(jnp.where(row == q, labels, 0.0), axis=0, keepdims=True)
            label = jnp.broadcast_to(label, (columns, channels)).astype(BF16)
            at = side * base + k * columns
            slots.append((label, block[at : at + columns, :]))
    for place in range(frames * 2):
        total = jnp.zeros((columns, channels), BF16)
        for label, values in slots:
            total = jnp.where(label == BF16(place), values, total)
        tile_ref[place // 2, first_row + place % 2] = total.astype(F32)


def gather_weight(blocks, wide_ref, core, high, low, share, base):
    side = len(blocks)
    p, q = walk(core, high, low)
    for j in range(side):
        for k in range(side):
            owner = chip_of(core, jnp.bitwise_xor(p, k), jnp.bitwise_xor(q, j), side)
            start = pl.multiple_of(owner * share, 8)
            values = blocks[j][k * base : (k + 1) * base, :].astype(F32)
            wide_ref[pl.ds(start, share), :] = values[:share]


def shifted(field):
    shape = field.shape
    column = lax.broadcasted_iota(jnp.int32, shape, len(shape) - 2)
    count = shape[-2]
    flat = field.reshape(-1, shape[-1])
    low = pltpu.roll(flat, 1, 0).reshape(shape)
    high = pltpu.roll(flat, flat.shape[0] - 1, 0).reshape(shape)
    low = jnp.where(column == 0, 0.0, low)
    high = jnp.where(column == count - 1, 0.0, high)
    return low.astype(BF16), field.astype(BF16), high.astype(BF16)


def spread(field, store, flip):
    rows = field.shape[1]
    columns = shifted(field)
    for b in range(3):
        for e in range(3):
            source = columns[2 - e] if flip else columns[e]
            offset = (1 - b) if flip else (b - 1)
            low = max(0, -offset)
            high = min(rows, rows - offset)
            piece = b * 3 + e
            store(low, high, piece, source[:, low + offset : high + offset])
            for row in range(rows):
                if not low <= row < high:
                    store(row, row + 1, piece, jnp.zeros_like(source[:, :1]))


def store_pieces(columns_ref):
    channels = columns_ref.shape[-1] // 9

    def store(low, high, piece, values):
        columns_ref[:, low:high, :, piece * channels : (piece + 1) * channels] = values

    return store


def spread_weight(wide_ref, out_ref, transposed):
    channels = wide_ref.shape[-1]
    for a in range(3):
        for piece in range(9):
            at = (a * 9 + piece) * channels
            values = wide_ref[at : at + channels, :].astype(BF16)
            frame = slice(a * channels, (a + 1) * channels)
            place = slice(piece * channels, (piece + 1) * channels)
            if transposed:
                out_ref[frame, place] = values
            else:
                out_ref[place, frame] = values


def conv(columns, w_ref, frames):
    channels = w_ref.shape[1] // 3
    product = jnp.dot(columns, w_ref[...], preferred_element_type=F32)
    product = product.reshape(frames, -1, 3 * channels)
    parts = [product[:, :, a * channels : (a + 1) * channels] for a in range(3)]
    out = []
    for t in range(frames):
        out.append(parts[0][max(t - 2, 0)] + parts[1][max(t - 1, 0)] + parts[2][t])
    return out


def conv_back(columns, wl_ref, frames):
    channels = wl_ref.shape[0] // 3
    nt = (((1,), (1,)), ((), ()))
    product = lax.dot_general(columns, wl_ref[...], nt, preferred_element_type=F32)
    product = product.reshape(frames, -1, 3 * channels)
    parts = [product[:, :, a * channels : (a + 1) * channels] for a in range(3)]
    out = []
    for t in range(frames):
        total = parts[2][t]
        for a in range(2):
            for source in range(frames):
                if max(source + a - 2, 0) == t:
                    total = total + parts[a][source]
        out.append(total)
    return out


def act_gradient(act, wl_ref, columns_ref, store):
    frames, rows, count, nine = columns_ref.shape
    hidden = conv_back(columns_ref[...].reshape(-1, nine), wl_ref, frames)
    for t in range(frames):
        value = act[t].astype(F32)
        sig = 1.0 / (1.0 + jnp.exp(-value))
        slope = sig * (1.0 + value * (1.0 - sig))
        store(t, (hidden[t].reshape(value.shape) * slope).astype(BF16))


def spread_chosen(of_core_zero, mine_ref, other_ref, out_ref, transposed):
    core = lax.axis_index("rows")
    own = (core == 0) if of_core_zero else (core != 0)

    @pl.when(own)
    def _():
        spread_weight(mine_ref, out_ref, transposed)

    @pl.when(jnp.logical_not(own))
    def _():
        spread_weight(other_ref, out_ref, transposed)


def prepare_kernel(length_ref, *refs, share):
    side = len(refs) - 5
    blocks, first_other = refs[:side], refs[side]
    tile_ref, wide_ref, out_grad_ref, columns_ref = refs[side + 1 :]
    core, high, low = position(side)
    frames, rows, columns, channels = out_grad_ref.shape
    band_rows = rows // 2
    _, q = walk(core, high, low)
    settle(blocks, tile_ref, 0, q, share)
    gather_weight(blocks, wide_ref, core, high, low, share, block_rows(share))
    end = side * (block_rows(share) + columns)
    band = (frames, band_rows, columns, channels)
    for block, owner in ((blocks[0], core), (first_other, 1 - core)):
        cot = block[end:, :].reshape(band)
        for t in range(frames):
            out_grad_ref[t, pl.ds(owner * band_rows, band_rows)] = jnp.where(
                t < length_ref[0], cot[t].astype(F32), 0.0
            ).astype(BF16)

    @pl.when(core == 0)
    def _():
        spread(out_grad_ref[...].astype(F32), store_pieces(columns_ref), True)


def prepare(length, blocks_mine, first_other, band, share):
    frames, band_rows, columns, channels = band
    field = (frames, 2 * band_rows, columns, channels)
    return pl.pallas_call(
        functools.partial(prepare_kernel, share=share),
        out_shape=[
            jax.ShapeDtypeStruct(band, F32),
            jax.ShapeDtypeStruct((27 * channels, channels), F32),
            jax.ShapeDtypeStruct(field, BF16),
            jax.ShapeDtypeStruct(field[:-1] + (9 * channels,), BF16),
        ],
        in_specs=scalars(1) + whole(len(blocks_mine) + 1),
        out_specs=whole(4),
        compiler_params=SMALL,
    )(length, *blocks_mine, first_other)


def unit_kernel(tile_mine, wide_mine, out_grad_ref, columns_ref, *refs, scale, side, share):
    blocks_other, refs = refs[:side], refs[side:]
    tile_ref, act_ref, act_grad_ref, wide_other = refs[:4]
    outs, refs = refs[4 : 4 + side], refs[4 + side :]
    w_ref, wl_ref, total_ref, x_scratch, left_ref = refs
    core, high, low = position(side)
    frames, rows, columns, channels = tile_ref.shape
    band_rows = rows // 2
    cells = frames * rows * columns
    nine = 9 * channels

    _, other_q = walk(1 - core, high, low)
    settle(blocks_other, tile_ref, (1 - core) * band_rows, other_q, share)
    tile_ref[:, pl.ds(core * band_rows, band_rows)] = tile_mine[...]
    gather_weight(blocks_other, wide_other, 1 - core, high, low, share, block_rows(share))
    spread_chosen(True, wide_mine, wide_other, w_ref, False)

    tile = tile_ref[...]
    first = tile / (1.0 + jnp.exp(-tile))
    spread(first, store_pieces(x_scratch.at[0]), False)
    act = conv(x_scratch[0].reshape(cells, nine), w_ref, frames)
    for t in range(frames):
        act_ref[t] = act[t].astype(BF16).reshape(rows, columns, channels)
    act = act_ref[...].astype(F32)
    second = act / (1.0 + jnp.exp(-act))
    spread(second, store_pieces(x_scratch.at[1]), False)

    @pl.when(core == 0)
    def _():
        def store(t, values):
            act_grad_ref[t] = values

        spread_weight(wide_other, wl_ref, True)
        act_gradient(act_ref, wl_ref, columns_ref, store)

    upstream = jnp.where(core == 0, act_grad_ref[...].astype(F32), out_grad_ref[...].astype(F32))
    upstream = upstream.reshape(frames, rows * columns, channels)
    turned = [upstream[t].T for t in range(frames)]
    for a in range(3):
        for t in range(frames):
            met = [turned[s] for s in range(frames) if max(s + a - 2, 0) == t]
            met = sum(met[1:], met[0]) if met else jnp.zeros_like(turned[0])
            frame = slice(a * channels, (a + 1) * channels)
            left_ref[frame, t * rows * columns : (t + 1) * rows * columns] = met.astype(BF16)
    product = jnp.dot(
        left_ref[...], x_scratch[core].reshape(cells, nine), preferred_element_type=F32
    )
    for a in range(3):
        for piece in range(9):
            at = (a * 9 + piece) * channels
            lanes = slice(piece * channels, (piece + 1) * channels)
            block = product[a * channels : (a + 1) * channels, lanes]
            total_ref[at : at + channels, :] = block.T * scale
    p, q = walk(core, high, low)
    for k in range(side):
        for j in range(side):
            owner = chip_of(core, j, jnp.bitwise_xor(q, k), side)
            start = pl.multiple_of(owner * share, 8)
            outs[k][j] = total_ref[pl.ds(start, share), :].astype(BF16)


def unit(prepared, blocks_other, scale, share):
    frames, rows, columns, channels = prepared[2].shape
    side = len(blocks_other)
    field = (frames, rows, columns, channels)
    cells = frames * rows * columns
    part = jax.ShapeDtypeStruct((side, share, channels), BF16)
    flops = 2 * 27 * channels * channels * cells * 3
    outs = pl.pallas_call(
        functools.partial(unit_kernel, scale=scale, side=side, share=share),
        out_shape=[
            jax.ShapeDtypeStruct(field, F32),
            jax.ShapeDtypeStruct(field, BF16),
            jax.ShapeDtypeStruct(field, BF16),
            jax.ShapeDtypeStruct((27 * channels, channels), F32),
        ]
        + [part] * side,
        in_specs=whole(len(prepared) + side),
        out_specs=whole(4 + side),
        scratch_shapes=[
            pltpu.VMEM((9 * channels, 3 * channels), BF16),
            pltpu.VMEM((3 * channels, 9 * channels), BF16),
            pltpu.VMEM((27 * channels, channels), F32),
            pltpu.VMEM((2, frames, rows, columns, 9 * channels), BF16),
            pltpu.VMEM((3 * channels, cells), BF16),
        ],
        compiler_params=pltpu.CompilerParams(vmem_limit_bytes=32 * 1024 * 1024),
        cost_estimate=pl.CostEstimate(flops=flops, bytes_accessed=4_000_000, transcendentals=0),
    )(*prepared, *blocks_other)
    tile, act, act_grad, wide_other = outs[:4]
    return (tile, act, prepared[2], act_grad, prepared[1], wide_other), outs[4:]


def finish_kernel(
    tile_ref,
    act_ref,
    out_grad_ref,
    act_grad_ref,
    wide_mine,
    wide_other,
    block_ref,
    grad_ref,
    w_ref,
    wl_ref,
    columns_ref,
    up_ref,
):
    frames, band_rows, columns, channels = block_ref.shape
    nine = 9 * channels
    core = lax.axis_index("rows")
    mine = pl.ds(core * band_rows, band_rows)
    shape = (band_rows, columns, channels)

    act = act_ref[...].astype(F32)
    second = act / (1.0 + jnp.exp(-act))
    spread(second, store_pieces(columns_ref), False)
    spread_chosen(False, wide_mine, wide_other, w_ref, False)
    out = conv(columns_ref[:, mine].reshape(-1, nine), w_ref, frames)
    for t in range(frames):
        block_ref[t] = (tile_ref[t, mine] + out[t].reshape(shape)).astype(BF16)

    @pl.when(core == 0)
    def _():
        up_ref[...] = act_grad_ref[...]

    @pl.when(core != 0)
    def _():
        def store(t, values):
            up_ref[t] = values

        spread_weight(wide_mine, wl_ref, True)
        spread(out_grad_ref[...].astype(F32), store_pieces(columns_ref), True)
        act_gradient(act_ref, wl_ref, columns_ref, store)

    spread(up_ref[...].astype(F32), store_pieces(columns_ref), True)
    spread_chosen(True, wide_mine, wide_other, wl_ref, True)
    out = conv_back(columns_ref[:, mine].reshape(-1, nine), wl_ref, frames)
    for t in range(frames):
        tile = tile_ref[t, mine]
        sig = 1.0 / (1.0 + jnp.exp(-tile))
        slope = sig * (1.0 + tile * (1.0 - sig))
        upstream = out_grad_ref[t, mine].astype(F32)
        grad_ref[t] = (upstream + out[t].reshape(shape) * slope).astype(BF16)


def finish(kept):
    frames, rows, columns, channels = kept[0].shape
    band = jax.ShapeDtypeStruct((frames, rows // 2, columns, channels), BF16)
    flops = 2 * 27 * channels * channels * frames * rows * columns
    return pl.pallas_call(
        finish_kernel,
        out_shape=[band] * 2,
        in_specs=whole(len(kept)),
        out_specs=whole(2),
        scratch_shapes=[
            pltpu.VMEM((9 * channels, 3 * channels), BF16),
            pltpu.VMEM((3 * channels, 9 * channels), BF16),
            pltpu.VMEM((frames, rows, columns, 9 * channels), BF16),
            pltpu.VMEM((frames, rows, columns, channels), BF16),
        ],
        compiler_params=pltpu.CompilerParams(vmem_limit_bytes=20 * 1024 * 1024),
        cost_estimate=pl.CostEstimate(flops=flops, bytes_accessed=2_000_000, transcendentals=0),
    )(*kept)


def total_of(refs, at):
    total = refs[0][at].astype(F32)
    for ref in refs[1:]:
        total = total + ref[at].astype(F32)
    return total


def middle_kernel(*refs):
    side = len(refs) // 2
    core, high, low = position(side)
    p, _ = walk(core, high, low)
    for k in range(side):
        refs[side + k][...] = total_of(refs[:side][::-1], jnp.bitwise_xor(p, k)).astype(BF16)


def middle(parts):
    side = len(parts)
    return pl.pallas_call(
        middle_kernel,
        out_shape=[jax.ShapeDtypeStruct(parts[0].shape[1:], BF16)] * side,
        in_specs=whole(side),
        out_specs=whole(side),
        compiler_params=SMALL,
    )(*parts[::-1])


def last_kernel(*refs):
    refs[-1][...] = total_of(refs[:-1][::-1], ...)


def last(parts):
    return pl.pallas_call(
        last_kernel,
        out_shape=jax.ShapeDtypeStruct(parts[0].shape, F32),
        in_specs=whole(len(parts)),
        out_specs=whole(1)[0],
        compiler_params=SMALL,
    )(*parts[::-1])


def body_pair(slabs, dest, pos, lengths, cot, w_first, w_second):
    wide_size = lax.axis_size("wide")
    side = math.isqrt(wide_size)
    core = lax.axis_index("rows")
    frames, band_rows, columns, channels = cot.shape[1:]
    share = w_first.shape[0]
    base = block_rows(share)

    def exchange(block):
        return lax.ppermute(block, "rows", [(0, 1), (1, 0)])

    def pairs(axes, k):
        both = []
        for chip in range(wide_size):
            high, low = chip // side, chip % side
            targets = ((high ^ k) * side + low, high * side + (low ^ k))
            both += [(chip * 2 + c, targets[axes[c]] * 2 + c) for c in range(2)]
        return both

    def send(blocks, axes):
        sent = [
            lax.ppermute(blocks[k], ("wide", "rows"), pairs(axes, k))
            for k in range(side - 1, 0, -1)
        ]
        return [blocks[0]] + sent[::-1]

    packed = pack(dest[0, 0], pos[0, 0], slabs[0, 0], w_first, w_second, side)
    _, *arrived = send(packed, (0, 1))
    kept_block, kept_cot = keep(packed[0], cot[0])
    relayed = relay(kept_cot, [kept_block, *arrived], columns, base)
    blocks_mine = send(relayed, (1, 0))
    blocks_other = [exchange(block) for block in blocks_mine]

    scale = 1.0 / math.sqrt(frames * band_rows * columns * 2 * wide_size)
    prepared = prepare(lengths, blocks_mine, blocks_other[0], cot.shape[1:], share)
    kept, parts = unit(prepared, blocks_other, scale, share)
    block_out, grad_input = finish(kept)

    arrived = send(parts, (1, 0))
    *arrived, block_out, grad_input = lax.optimization_barrier((*arrived, block_out, grad_input))
    total = last(send(middle(arrived), (0, 1)))
    total_other = exchange(total)
    share_first = jnp.where(core == 0, total, total_other)
    share_second = jnp.where(core == 0, total_other, total)
    return (block_out[None], grad_input[None], share_first, share_second)


def solution(mesh):
    side = math.isqrt(mesh.shape["wide"])
    square = side * side == mesh.shape["wide"] and side & (side - 1) == 0
    body = body_pair if mesh.shape["rows"] == 2 and square else body_general
    return jax.shard_map(
        body,
        mesh=mesh,
        in_specs=(
            P("wide", "rows", None, None, None),
            P("wide", "rows", None),
            P("wide", "rows", None),
            P("wide"),
            P("wide", None, "rows", None, None),
            P("wide", None),
            P("wide", None),
        ),
        out_specs=(
            P("wide", None, "rows", None, None),
            P("wide", None, "rows", None, None),
            P("wide", None),
            P("wide", None),
        ),
        check_vma=False,
    )
```

```python
import functools
import math

import jax
import jax.numpy as jnp
from jax import lax
from jax.experimental import pallas as pl
from jax.experimental.pallas import tpu as pltpu
from jax.sharding import PartitionSpec as P

BF16 = jnp.bfloat16
F32 = jnp.float32
SMALL = pltpu.CompilerParams(vmem_limit_bytes=8 * 1024 * 1024)


def with_halo(block, sides, width):
    for axis, dim in sides:
        count = lax.axis_size(axis)
        forward = [(i, i + 1) for i in range(count - 1)]
        backward = [(target, source) for source, target in forward]
        low = lax.ppermute(
            lax.slice_in_dim(block, block.shape[dim] - width, None, axis=dim), axis, forward
        )
        high = lax.ppermute(lax.slice_in_dim(block, 0, width, axis=dim), axis, backward)
        block = jnp.concatenate([low, block, high], axis=dim)
    return block


def silu_slope(values):
    sig = jax.nn.sigmoid(values)
    return sig * (1.0 + values * (1.0 - sig))


def conv_forward(extended, kernel):
    padded = jnp.concatenate([extended[:1], extended[:1], extended], axis=0)
    result = lax.conv_general_dilated(
        padded[None],
        kernel,
        (1, 1, 1),
        ((0, 0), (0, 0), (1, 1)),
        dimension_numbers=("NDHWC", "DHWIO", "NDHWC"),
        preferred_element_type=jnp.float32,
    )
    return result[0]


def conv_weight_grad(extended, upstream):
    padded = jnp.concatenate([extended[:1], extended[:1], extended], axis=0)
    result = lax.conv_general_dilated(
        padded[None],
        upstream[None],
        (1, 1, 1),
        ((0, 0), (0, 0), (1, 1)),
        dimension_numbers=("CDHWN", "IDHWO", "NDHWC"),
        preferred_element_type=jnp.float32,
    )
    channels = extended.shape[-1]
    return jnp.transpose(result, (1, 2, 3, 0, 4)).reshape(27 * channels, upstream.shape[-1])


def conv_data_grad(upstream_ext, kernel):
    padded = jnp.pad(upstream_ext, ((2, 2), (0, 0), (0, 0), (0, 0)))
    flipped = kernel[::-1, ::-1, ::-1]
    result = lax.conv_general_dilated(
        padded[None],
        flipped,
        (1, 1, 1),
        ((0, 0), (0, 0), (1, 1)),
        dimension_numbers=("NDHWC", "DHWOI", "NDHWC"),
        preferred_element_type=jnp.float32,
    )[0]
    head = (result[0] + result[1] + result[2])[None]
    return jnp.concatenate([head, result[3:]], axis=0)


def body_general(slabs, dest, pos, lengths, cot, w_first, w_second):
    wide_size = lax.axis_size("wide")
    band_count = lax.axis_size("rows")
    slab_count = slabs.shape[2]
    columns = slabs.shape[3]
    channels = slabs.shape[4]
    frames = cot.shape[1]
    band_rows = cot.shape[2]
    capacity = -(-slab_count // wide_size)
    slot_count = wide_size * capacity
    targets = dest[0, 0]
    places = pos[0, 0]
    ranking = jnp.arange(slab_count, dtype=jnp.int32)
    earlier = (targets[None, :] == targets[:, None]) & (ranking[None, :] < ranking[:, None])
    slab_rank = jnp.sum(earlier.astype(jnp.int32), axis=1)
    slot_of = targets * capacity + slab_rank
    placing = slot_of[None, :] == jnp.arange(slot_count, dtype=jnp.int32)[:, None]
    flat_slabs = slabs[0, 0].reshape(slab_count, columns * channels)
    outgoing = jnp.dot(placing.astype(jnp.bfloat16), flat_slabs, preferred_element_type=jnp.float32)
    outgoing = outgoing.astype(jnp.bfloat16).reshape(wide_size, capacity, columns * channels)
    labels = jnp.sum(jnp.where(placing, places[None, :] + 1, 0), axis=1) - 1
    labels = labels.reshape(wide_size, capacity)
    arrived, arrived_places = (
        lax.all_to_all(outgoing, "wide", split_axis=0, concat_axis=0, tiled=True),
        lax.all_to_all(labels, "wide", split_axis=0, concat_axis=0, tiled=True),
    )
    settle = (
        arrived_places.reshape(slot_count)[None, :]
        == jnp.arange(slab_count, dtype=jnp.int32)[:, None]
    )
    tile = jnp.dot(
        settle.astype(jnp.bfloat16),
        arrived.reshape(slot_count, columns * channels),
        preferred_element_type=jnp.float32,
    )
    tile = tile.astype(jnp.bfloat16).reshape(frames, band_rows, columns, channels)
    full_first, full_second = (
        lax.all_gather(w_first, "wide", axis=0, tiled=True),
        lax.all_gather(w_second, "wide", axis=0, tiled=True),
    )
    kernel_first = full_first.reshape(3, 3, 3, channels, channels)
    kernel_second = full_second.reshape(3, 3, 3, channels, channels)
    tile_wide = tile.astype(jnp.float32)
    first = jax.nn.silu(tile_wide).astype(jnp.bfloat16)
    first_ext = with_halo(first, (("rows", 1),), 1)
    act = conv_forward(first_ext, kernel_first).astype(jnp.bfloat16)
    second = jax.nn.silu(act.astype(jnp.float32)).astype(jnp.bfloat16)
    second_ext = with_halo(second, (("rows", 1),), 1)
    block_out = (tile_wide + conv_forward(second_ext, kernel_second)).astype(jnp.bfloat16)
    live = (jnp.arange(frames, dtype=jnp.int32) < lengths[0])[:, None, None, None]
    out_grad = jnp.where(live, cot[0], jnp.zeros_like(cot[0]))
    out_grad_ext = with_halo(out_grad, (("rows", 1),), 1)
    weight_second = conv_weight_grad(second_ext, out_grad)
    hidden_grad = conv_data_grad(out_grad_ext, kernel_second)
    act_grad = (hidden_grad * silu_slope(act.astype(jnp.float32))).astype(jnp.bfloat16)
    act_grad_ext = with_halo(act_grad, (("rows", 1),), 1)
    weight_first = conv_weight_grad(first_ext, act_grad)
    first_grad = conv_data_grad(act_grad_ext, kernel_first)
    grad_input = (out_grad.astype(jnp.float32) + first_grad * silu_slope(tile_wide)).astype(
        jnp.bfloat16
    )
    scale = 1.0 / math.sqrt(frames * band_rows * columns * band_count * wide_size)
    weight_first = weight_first * scale
    weight_second = weight_second * scale
    total_first, total_second = (
        lax.psum(weight_first.astype(jnp.bfloat16), "rows").astype(jnp.float32),
        lax.psum(weight_second.astype(jnp.bfloat16), "rows").astype(jnp.float32),
    )
    share_first, share_second = (
        lax.psum_scatter(total_first, "wide", scatter_dimension=0, tiled=True),
        lax.psum_scatter(total_second, "wide", scatter_dimension=0, tiled=True),
    )
    return (block_out[None], grad_input[None], share_first, share_second)


def whole(count):
    return [pl.BlockSpec(memory_space=pltpu.VMEM)] * count


def scalars(count):
    return [pl.BlockSpec(memory_space=pltpu.SMEM)] * count


def position(side):
    core = lax.axis_index("rows")
    wide = lax.axis_index("wide")
    high, low = wide // side, lax.rem(wide, side)
    return core, high, low


def walk(core, high, low):
    return jnp.where(core == 0, high, low), jnp.where(core == 0, low, high)


def chip_of(core, p, q, side):
    high, low = walk(core, p, q)
    return high * side + low


def block_rows(share):
    return -(-(share + 8) // 16) * 16


def pack_kernel(dest_ref, pos_ref, slabs_hbm, first_hbm, second_hbm, *refs):
    side = len(refs) - 4
    out_refs = refs[:side]
    slabs_ref, own_ref, block_ref, sem = refs[side:]
    core, high, low = position(side)
    p, _ = walk(core, high, low)
    count, columns, channels = slabs_ref.shape
    share = own_ref.shape[0]
    base = block_rows(share)
    load_slabs = pltpu.make_async_copy(slabs_hbm, slabs_ref, sem.at[0])
    load_first = pltpu.make_async_copy(first_hbm, own_ref, sem.at[1])
    load_second = pltpu.make_async_copy(second_hbm, own_ref, sem.at[1])
    load_slabs.start()

    @pl.when(core == 0)
    def _():
        load_first.start()

    @pl.when(core != 0)
    def _():
        load_second.start()

    block_ref[...] = jnp.zeros(block_ref.shape, BF16)
    row = lax.broadcasted_iota(jnp.int32, (base - share, channels), 0)
    labels = [jnp.full((base - share, channels), -1.0, F32) for _ in range(side)]
    steps, slots = [], []
    for s in range(count):
        p_to, q_to = walk(core, dest_ref[s] // side, lax.rem(dest_ref[s], side))
        steps.append(jnp.bitwise_xor(p, p_to))
        slots.append(q_to)
        place = pos_ref[s].astype(F32)
        for k in range(side):
            hit = jnp.where(steps[s] == k, q_to, -1)
            labels[k] = jnp.where(row == hit, place, labels[k])
    load_slabs.wait()
    for s in range(count):
        start = pl.multiple_of(slots[s] * columns, columns)
        block_ref[steps[s], pl.ds(start, columns), :] = slabs_ref[s]
    for k in range(side):
        out_refs[k][base:, :] = block_ref[k]
    load_first.wait()
    own = own_ref[...].astype(F32)
    for k in range(side):
        out_refs[k][:base, :] = jnp.concatenate([own, labels[k]], axis=0).astype(BF16)


def pack(dest, pos, slabs, first, second, side):
    count, columns, channels = slabs.shape
    rows = block_rows(first.shape[0]) + side * columns
    return pl.pallas_call(
        pack_kernel,
        out_shape=[jax.ShapeDtypeStruct((rows, channels), BF16)] * side,
        in_specs=scalars(2) + [pl.BlockSpec(memory_space=pltpu.HBM)] * 3,
        out_specs=whole(side),
        scratch_shapes=[
            pltpu.VMEM(slabs.shape, BF16),
            pltpu.VMEM(first.shape, BF16),
            pltpu.VMEM((side, side * columns, channels), BF16),
            pltpu.SemaphoreType.DMA((2,)),
        ],
    )(dest, pos, slabs, first, second)


def keep_kernel(*refs):
    half = len(refs) // 2
    for source, target in zip(refs[:half], refs[half:]):
        target[...] = source[...]


def keep(*blocks):
    return pl.pallas_call(
        keep_kernel,
        out_shape=[jax.ShapeDtypeStruct(block.shape, block.dtype) for block in blocks],
        in_specs=whole(len(blocks)),
        out_specs=whole(len(blocks)),
        compiler_params=SMALL,
    )(*blocks)


def relay_kernel(cot_ref, *refs, columns, base):
    side = len(refs) // 2
    ins, outs = refs[:side][::-1], refs[side:]
    core, high, low = position(side)
    _, q = walk(core, high, low)
    for j in range(side):
        start = pl.multiple_of(base + jnp.bitwise_xor(q, j) * columns, 16)
        for k in range(side):
            outs[j][k * base : (k + 1) * base, :] = ins[k][:base, :]
            at = side * base + k * columns
            outs[j][at : at + columns, :] = ins[k][pl.ds(start, columns), :]
    outs[0][side * (base + columns) :, :] = cot_ref[...].reshape(-1, cot_ref.shape[-1])


def relay(cot, ins, columns, base):
    side = len(ins)
    channels = ins[0].shape[1]
    rows = side * (base + columns)
    extra = cot.size // channels
    return pl.pallas_call(
        functools.partial(relay_kernel, columns=columns, base=base),
        out_shape=[jax.ShapeDtypeStruct((rows + extra, channels), BF16)]
        + [jax.ShapeDtypeStruct((rows, channels), BF16)] * (side - 1),
        in_specs=whole(side + 1),
        out_specs=whole(side),
        compiler_params=SMALL,
    )(cot, *ins[::-1])


def settle(blocks, tile_ref, first_row, q, share):
    side = len(blocks)
    base = block_rows(share)
    frames, _, columns, channels = tile_ref.shape
    row = lax.broadcasted_iota(jnp.int32, (base - share, channels), 0)
    slots = []
    for block in blocks:
        for k in range(side):
            labels = block[k * base : (k + 1) * base, :].astype(F32)[share:]
            label = jnp.sum(jnp.where(row == q, labels, 0.0), axis=0, keepdims=True)
            label = jnp.broadcast_to(label, (columns, channels)).astype(BF16)
            at = side * base + k * columns
            slots.append((label, block[at : at + columns, :]))
    for place in range(frames * 2):
        total = jnp.zeros((columns, channels), BF16)
        for label, values in slots:
            total = jnp.where(label == BF16(place), values, total)
        tile_ref[place // 2, first_row + place % 2] = total.astype(F32)


def gather_weight(blocks, wide_ref, core, high, low, share, base):
    side = len(blocks)
    p, q = walk(core, high, low)
    for j in range(side):
        for k in range(side):
            owner = chip_of(core, jnp.bitwise_xor(p, k), jnp.bitwise_xor(q, j), side)
            start = pl.multiple_of(owner * share, 8)
            values = blocks[j][k * base : (k + 1) * base, :].astype(F32)
            wide_ref[pl.ds(start, share), :] = values[:share]


def shifted(field):
    shape = field.shape
    column = lax.broadcasted_iota(jnp.int32, shape, len(shape) - 2)
    count = shape[-2]
    flat = field.reshape(-1, shape[-1])
    low = pltpu.roll(flat, 1, 0).reshape(shape)
    high = pltpu.roll(flat, flat.shape[0] - 1, 0).reshape(shape)
    low = jnp.where(column == 0, 0.0, low)
    high = jnp.where(column == count - 1, 0.0, high)
    return low.astype(BF16), field.astype(BF16), high.astype(BF16)


def spread(field, store, flip):
    rows = field.shape[1]
    columns = shifted(field)
    for b in range(3):
        for e in range(3):
            source = columns[2 - e] if flip else columns[e]
            offset = (1 - b) if flip else (b - 1)
            low = max(0, -offset)
            high = min(rows, rows - offset)
            piece = b * 3 + e
            store(low, high, piece, source[:, low + offset : high + offset])
            for row in range(rows):
                if not low <= row < high:
                    store(row, row + 1, piece, jnp.zeros_like(source[:, :1]))


def store_pieces(columns_ref):
    channels = columns_ref.shape[-1] // 9

    def store(low, high, piece, values):
        columns_ref[:, low:high, :, piece * channels : (piece + 1) * channels] = values

    return store


def spread_weight(wide_ref, out_ref, transposed):
    channels = wide_ref.shape[-1]
    for a in range(3):
        for piece in range(9):
            at = (a * 9 + piece) * channels
            values = wide_ref[at : at + channels, :].astype(BF16)
            frame = slice(a * channels, (a + 1) * channels)
            place = slice(piece * channels, (piece + 1) * channels)
            if transposed:
                out_ref[frame, place] = values
            else:
                out_ref[place, frame] = values


def conv(columns, w_ref, frames):
    channels = w_ref.shape[1] // 3
    product = jnp.dot(columns, w_ref[...], preferred_element_type=F32)
    product = product.reshape(frames, -1, 3 * channels)
    parts = [product[:, :, a * channels : (a + 1) * channels] for a in range(3)]
    out = []
    for t in range(frames):
        out.append(parts[0][max(t - 2, 0)] + parts[1][max(t - 1, 0)] + parts[2][t])
    return out


def conv_back(columns, wl_ref, frames):
    channels = wl_ref.shape[0] // 3
    nt = (((1,), (1,)), ((), ()))
    product = lax.dot_general(columns, wl_ref[...], nt, preferred_element_type=F32)
    product = product.reshape(frames, -1, 3 * channels)
    parts = [product[:, :, a * channels : (a + 1) * channels] for a in range(3)]
    out = []
    for t in range(frames):
        total = parts[2][t]
        for a in range(2):
            for source in range(frames):
                if max(source + a - 2, 0) == t:
                    total = total + parts[a][source]
        out.append(total)
    return out


def act_gradient(act, wl_ref, columns_ref, store):
    frames, rows, count, nine = columns_ref.shape
    hidden = conv_back(columns_ref[...].reshape(-1, nine), wl_ref, frames)
    for t in range(frames):
        value = act[t].astype(F32)
        sig = 1.0 / (1.0 + jnp.exp(-value))
        slope = sig * (1.0 + value * (1.0 - sig))
        store(t, (hidden[t].reshape(value.shape) * slope).astype(BF16))


def spread_chosen(of_core_zero, mine_ref, other_ref, out_ref, transposed):
    core = lax.axis_index("rows")
    own = (core == 0) if of_core_zero else (core != 0)

    @pl.when(own)
    def _():
        spread_weight(mine_ref, out_ref, transposed)

    @pl.when(jnp.logical_not(own))
    def _():
        spread_weight(other_ref, out_ref, transposed)


def prepare_kernel(length_ref, *refs, share):
    side = len(refs) - 5
    blocks, first_other = refs[:side], refs[side]
    tile_ref, wide_ref, out_grad_ref, columns_ref = refs[side + 1 :]
    core, high, low = position(side)
    frames, rows, columns, channels = out_grad_ref.shape
    band_rows = rows // 2
    _, q = walk(core, high, low)
    settle(blocks, tile_ref, 0, q, share)
    gather_weight(blocks, wide_ref, core, high, low, share, block_rows(share))
    end = side * (block_rows(share) + columns)
    band = (frames, band_rows, columns, channels)
    for block, owner in ((blocks[0], core), (first_other, 1 - core)):
        cot = block[end:, :].reshape(band)
        for t in range(frames):
            out_grad_ref[t, pl.ds(owner * band_rows, band_rows)] = jnp.where(
                t < length_ref[0], cot[t].astype(F32), 0.0
            ).astype(BF16)

    @pl.when(core == 0)
    def _():
        spread(out_grad_ref[...].astype(F32), store_pieces(columns_ref), True)


def prepare(length, blocks_mine, first_other, band, share):
    frames, band_rows, columns, channels = band
    field = (frames, 2 * band_rows, columns, channels)
    return pl.pallas_call(
        functools.partial(prepare_kernel, share=share),
        out_shape=[
            jax.ShapeDtypeStruct(band, F32),
            jax.ShapeDtypeStruct((27 * channels, channels), F32),
            jax.ShapeDtypeStruct(field, BF16),
            jax.ShapeDtypeStruct(field[:-1] + (9 * channels,), BF16),
        ],
        in_specs=scalars(1) + whole(len(blocks_mine) + 1),
        out_specs=whole(4),
        compiler_params=SMALL,
    )(length, *blocks_mine, first_other)


def unit_kernel(tile_mine, wide_mine, out_grad_ref, columns_ref, *refs, scale, side, share):
    blocks_other, refs = refs[:side], refs[side:]
    tile_ref, act_ref, act_grad_ref, wide_other = refs[:4]
    outs, refs = refs[4 : 4 + side], refs[4 + side :]
    w_ref, wl_ref, total_ref, x_scratch, right_ref = refs
    core, high, low = position(side)
    frames, rows, columns, channels = tile_ref.shape
    band_rows = rows // 2
    cells = frames * rows * columns
    nine = 9 * channels

    _, other_q = walk(1 - core, high, low)
    settle(blocks_other, tile_ref, (1 - core) * band_rows, other_q, share)
    tile_ref[:, pl.ds(core * band_rows, band_rows)] = tile_mine[...]
    gather_weight(blocks_other, wide_other, 1 - core, high, low, share, block_rows(share))
    spread_chosen(True, wide_mine, wide_other, w_ref, False)

    tile = tile_ref[...]
    first = tile / (1.0 + jnp.exp(-tile))
    spread(first, store_pieces(x_scratch.at[0]), False)
    act = conv(x_scratch[0].reshape(cells, nine), w_ref, frames)
    for t in range(frames):
        act_ref[t] = act[t].astype(BF16).reshape(rows, columns, channels)
    act = act_ref[...].astype(F32)
    second = act / (1.0 + jnp.exp(-act))
    spread(second, store_pieces(x_scratch.at[1]), False)

    @pl.when(core == 0)
    def _():
        def store(t, values):
            act_grad_ref[t] = values

        spread_weight(wide_other, wl_ref, True)
        act_gradient(act_ref, wl_ref, columns_ref, store)

    upstream = jnp.where(core == 0, act_grad_ref[...].astype(F32), out_grad_ref[...].astype(F32))
    upstream = upstream.reshape(frames, rows * columns, channels)
    for a in range(3):
        for t in range(frames):
            met = [upstream[s] for s in range(frames) if max(s + a - 2, 0) == t]
            met = sum(met[1:], met[0]) if met else jnp.zeros_like(upstream[0])
            frame = slice(a * channels, (a + 1) * channels)
            right_ref[t * rows * columns : (t + 1) * rows * columns, frame] = met.astype(BF16)
    product = lax.dot_general(
        x_scratch[core].reshape(cells, nine),
        right_ref[...],
        (((0,), (0,)), ((), ())),
        preferred_element_type=F32,
    )
    for a in range(3):
        for piece in range(9):
            at = (a * 9 + piece) * channels
            place = slice(piece * channels, (piece + 1) * channels)
            block = product[place, a * channels : (a + 1) * channels]
            total_ref[at : at + channels, :] = block * scale
    p, q = walk(core, high, low)
    for k in range(side):
        for j in range(side):
            owner = chip_of(core, j, jnp.bitwise_xor(q, k), side)
            start = pl.multiple_of(owner * share, 8)
            outs[k][j] = total_ref[pl.ds(start, share), :].astype(BF16)


def unit(prepared, blocks_other, scale, share):
    frames, rows, columns, channels = prepared[2].shape
    side = len(blocks_other)
    field = (frames, rows, columns, channels)
    cells = frames * rows * columns
    part = jax.ShapeDtypeStruct((side, share, channels), BF16)
    flops = 2 * 27 * channels * channels * cells * 3
    outs = pl.pallas_call(
        functools.partial(unit_kernel, scale=scale, side=side, share=share),
        out_shape=[
            jax.ShapeDtypeStruct(field, F32),
            jax.ShapeDtypeStruct(field, BF16),
            jax.ShapeDtypeStruct(field, BF16),
            jax.ShapeDtypeStruct((27 * channels, channels), F32),
        ]
        + [part] * side,
        in_specs=whole(len(prepared) + side),
        out_specs=whole(4 + side),
        scratch_shapes=[
            pltpu.VMEM((9 * channels, 3 * channels), BF16),
            pltpu.VMEM((3 * channels, 9 * channels), BF16),
            pltpu.VMEM((27 * channels, channels), F32),
            pltpu.VMEM((2, frames, rows, columns, 9 * channels), BF16),
            pltpu.VMEM((cells, 3 * channels), BF16),
        ],
        compiler_params=pltpu.CompilerParams(vmem_limit_bytes=32 * 1024 * 1024),
        cost_estimate=pl.CostEstimate(flops=flops, bytes_accessed=4_000_000, transcendentals=0),
    )(*prepared, *blocks_other)
    tile, act, act_grad, wide_other = outs[:4]
    return (tile, act, prepared[2], act_grad, prepared[1], wide_other), outs[4:]


def finish_kernel(
    tile_ref,
    act_ref,
    out_grad_ref,
    act_grad_ref,
    wide_mine,
    wide_other,
    block_ref,
    grad_ref,
    w_ref,
    wl_ref,
    columns_ref,
    up_ref,
):
    frames, band_rows, columns, channels = block_ref.shape
    nine = 9 * channels
    core = lax.axis_index("rows")
    mine = pl.ds(core * band_rows, band_rows)
    shape = (band_rows, columns, channels)

    act = act_ref[...].astype(F32)
    second = act / (1.0 + jnp.exp(-act))
    spread(second, store_pieces(columns_ref), False)
    spread_chosen(False, wide_mine, wide_other, w_ref, False)
    out = conv(columns_ref[:, mine].reshape(-1, nine), w_ref, frames)
    for t in range(frames):
        block_ref[t] = (tile_ref[t, mine] + out[t].reshape(shape)).astype(BF16)

    @pl.when(core == 0)
    def _():
        up_ref[...] = act_grad_ref[...]

    @pl.when(core != 0)
    def _():
        def store(t, values):
            up_ref[t] = values

        spread_weight(wide_mine, wl_ref, True)
        spread(out_grad_ref[...].astype(F32), store_pieces(columns_ref), True)
        act_gradient(act_ref, wl_ref, columns_ref, store)

    spread(up_ref[...].astype(F32), store_pieces(columns_ref), True)
    spread_chosen(True, wide_mine, wide_other, wl_ref, True)
    out = conv_back(columns_ref[:, mine].reshape(-1, nine), wl_ref, frames)
    for t in range(frames):
        tile = tile_ref[t, mine]
        sig = 1.0 / (1.0 + jnp.exp(-tile))
        slope = sig * (1.0 + tile * (1.0 - sig))
        upstream = out_grad_ref[t, mine].astype(F32)
        grad_ref[t] = (upstream + out[t].reshape(shape) * slope).astype(BF16)


def finish(kept):
    frames, rows, columns, channels = kept[0].shape
    band = jax.ShapeDtypeStruct((frames, rows // 2, columns, channels), BF16)
    flops = 2 * 27 * channels * channels * frames * rows * columns
    return pl.pallas_call(
        finish_kernel,
        out_shape=[band] * 2,
        in_specs=whole(len(kept)),
        out_specs=whole(2),
        scratch_shapes=[
            pltpu.VMEM((9 * channels, 3 * channels), BF16),
            pltpu.VMEM((3 * channels, 9 * channels), BF16),
            pltpu.VMEM((frames, rows, columns, 9 * channels), BF16),
            pltpu.VMEM((frames, rows, columns, channels), BF16),
        ],
        compiler_params=pltpu.CompilerParams(vmem_limit_bytes=20 * 1024 * 1024),
        cost_estimate=pl.CostEstimate(flops=flops, bytes_accessed=2_000_000, transcendentals=0),
    )(*kept)


def total_of(refs, at):
    total = refs[0][at].astype(F32)
    for ref in refs[1:]:
        total = total + ref[at].astype(F32)
    return total


def middle_kernel(*refs):
    side = len(refs) // 2
    core, high, low = position(side)
    p, _ = walk(core, high, low)
    for k in range(side):
        refs[side + k][...] = total_of(refs[:side][::-1], jnp.bitwise_xor(p, k)).astype(BF16)


def middle(parts):
    side = len(parts)
    return pl.pallas_call(
        middle_kernel,
        out_shape=[jax.ShapeDtypeStruct(parts[0].shape[1:], BF16)] * side,
        in_specs=whole(side),
        out_specs=whole(side),
        compiler_params=SMALL,
    )(*parts[::-1])


def last_kernel(*refs):
    refs[-1][...] = total_of(refs[:-1][::-1], ...)


def last(parts):
    return pl.pallas_call(
        last_kernel,
        out_shape=jax.ShapeDtypeStruct(parts[0].shape, F32),
        in_specs=whole(len(parts)),
        out_specs=whole(1)[0],
        compiler_params=SMALL,
    )(*parts[::-1])


def body_pair(slabs, dest, pos, lengths, cot, w_first, w_second):
    wide_size = lax.axis_size("wide")
    side = math.isqrt(wide_size)
    core = lax.axis_index("rows")
    frames, band_rows, columns, channels = cot.shape[1:]
    share = w_first.shape[0]
    base = block_rows(share)

    def exchange(block):
        return lax.ppermute(block, "rows", [(0, 1), (1, 0)])

    def pairs(axes, k):
        both = []
        for chip in range(wide_size):
            high, low = chip // side, chip % side
            targets = ((high ^ k) * side + low, high * side + (low ^ k))
            both += [(chip * 2 + c, targets[axes[c]] * 2 + c) for c in range(2)]
        return both

    def send(blocks, axes):
        sent = [
            lax.ppermute(blocks[k], ("wide", "rows"), pairs(axes, k))
            for k in range(side - 1, 0, -1)
        ]
        return [blocks[0]] + sent[::-1]

    packed = pack(dest[0, 0], pos[0, 0], slabs[0, 0], w_first, w_second, side)
    _, *arrived = send(packed, (0, 1))
    kept_block, kept_cot = keep(packed[0], cot[0])
    relayed = relay(kept_cot, [kept_block, *arrived], columns, base)
    blocks_mine = send(relayed, (1, 0))
    own_block, _ = lax.optimization_barrier((blocks_mine[0], blocks_mine[1]))
    blocks_other = [exchange(block) for block in (own_block, *blocks_mine[1:])]

    scale = 1.0 / math.sqrt(frames * band_rows * columns * 2 * wide_size)
    prepared = prepare(lengths, blocks_mine, blocks_other[0], cot.shape[1:], share)
    kept, parts = unit(prepared, blocks_other, scale, share)
    block_out, grad_input = finish(kept)

    arrived = send(parts, (1, 0))
    *arrived, block_out, grad_input = lax.optimization_barrier((*arrived, block_out, grad_input))
    total = last(send(middle(arrived), (0, 1)))
    total_other = exchange(total)
    share_first = jnp.where(core == 0, total, total_other)
    share_second = jnp.where(core == 0, total_other, total)
    return (block_out[None], grad_input[None], share_first, share_second)


def solution(mesh):
    side = math.isqrt(mesh.shape["wide"])
    square = side * side == mesh.shape["wide"] and side & (side - 1) == 0
    body = body_pair if mesh.shape["rows"] == 2 and square else body_general
    return jax.shard_map(
        body,
        mesh=mesh,
        in_specs=(
            P("wide", "rows", None, None, None),
            P("wide", "rows", None),
            P("wide", "rows", None),
            P("wide"),
            P("wide", None, "rows", None, None),
            P("wide", None),
            P("wide", None),
        ),
        out_specs=(
            P("wide", None, "rows", None, None),
            P("wide", None, "rows", None, None),
            P("wide", None),
            P("wide", None),
        ),
        check_vma=False,
    )
```

```python
import functools
import math

import jax
import jax.numpy as jnp
from jax import lax
from jax.experimental import pallas as pl
from jax.experimental.pallas import tpu as pltpu
from jax.sharding import PartitionSpec as P

BF16 = jnp.bfloat16
F32 = jnp.float32
SMALL = pltpu.CompilerParams(vmem_limit_bytes=8 * 1024 * 1024)


def with_halo(block, sides, width):
    for axis, dim in sides:
        count = lax.axis_size(axis)
        forward = [(i, i + 1) for i in range(count - 1)]
        backward = [(target, source) for source, target in forward]
        low = lax.ppermute(
            lax.slice_in_dim(block, block.shape[dim] - width, None, axis=dim), axis, forward
        )
        high = lax.ppermute(lax.slice_in_dim(block, 0, width, axis=dim), axis, backward)
        block = jnp.concatenate([low, block, high], axis=dim)
    return block


def silu_slope(values):
    sig = jax.nn.sigmoid(values)
    return sig * (1.0 + values * (1.0 - sig))


def conv_forward(extended, kernel):
    padded = jnp.concatenate([extended[:1], extended[:1], extended], axis=0)
    result = lax.conv_general_dilated(
        padded[None],
        kernel,
        (1, 1, 1),
        ((0, 0), (0, 0), (1, 1)),
        dimension_numbers=("NDHWC", "DHWIO", "NDHWC"),
        preferred_element_type=jnp.float32,
    )
    return result[0]


def conv_weight_grad(extended, upstream):
    padded = jnp.concatenate([extended[:1], extended[:1], extended], axis=0)
    result = lax.conv_general_dilated(
        padded[None],
        upstream[None],
        (1, 1, 1),
        ((0, 0), (0, 0), (1, 1)),
        dimension_numbers=("CDHWN", "IDHWO", "NDHWC"),
        preferred_element_type=jnp.float32,
    )
    channels = extended.shape[-1]
    return jnp.transpose(result, (1, 2, 3, 0, 4)).reshape(27 * channels, upstream.shape[-1])


def conv_data_grad(upstream_ext, kernel):
    padded = jnp.pad(upstream_ext, ((2, 2), (0, 0), (0, 0), (0, 0)))
    flipped = kernel[::-1, ::-1, ::-1]
    result = lax.conv_general_dilated(
        padded[None],
        flipped,
        (1, 1, 1),
        ((0, 0), (0, 0), (1, 1)),
        dimension_numbers=("NDHWC", "DHWOI", "NDHWC"),
        preferred_element_type=jnp.float32,
    )[0]
    head = (result[0] + result[1] + result[2])[None]
    return jnp.concatenate([head, result[3:]], axis=0)


def body_general(slabs, dest, pos, lengths, cot, w_first, w_second):
    wide_size = lax.axis_size("wide")
    band_count = lax.axis_size("rows")
    slab_count = slabs.shape[2]
    columns = slabs.shape[3]
    channels = slabs.shape[4]
    frames = cot.shape[1]
    band_rows = cot.shape[2]
    capacity = -(-slab_count // wide_size)
    slot_count = wide_size * capacity
    targets = dest[0, 0]
    places = pos[0, 0]
    ranking = jnp.arange(slab_count, dtype=jnp.int32)
    earlier = (targets[None, :] == targets[:, None]) & (ranking[None, :] < ranking[:, None])
    slab_rank = jnp.sum(earlier.astype(jnp.int32), axis=1)
    slot_of = targets * capacity + slab_rank
    placing = slot_of[None, :] == jnp.arange(slot_count, dtype=jnp.int32)[:, None]
    flat_slabs = slabs[0, 0].reshape(slab_count, columns * channels)
    outgoing = jnp.dot(placing.astype(jnp.bfloat16), flat_slabs, preferred_element_type=jnp.float32)
    outgoing = outgoing.astype(jnp.bfloat16).reshape(wide_size, capacity, columns * channels)
    labels = jnp.sum(jnp.where(placing, places[None, :] + 1, 0), axis=1) - 1
    labels = labels.reshape(wide_size, capacity)
    arrived, arrived_places = (
        lax.all_to_all(outgoing, "wide", split_axis=0, concat_axis=0, tiled=True),
        lax.all_to_all(labels, "wide", split_axis=0, concat_axis=0, tiled=True),
    )
    settle = (
        arrived_places.reshape(slot_count)[None, :]
        == jnp.arange(slab_count, dtype=jnp.int32)[:, None]
    )
    tile = jnp.dot(
        settle.astype(jnp.bfloat16),
        arrived.reshape(slot_count, columns * channels),
        preferred_element_type=jnp.float32,
    )
    tile = tile.astype(jnp.bfloat16).reshape(frames, band_rows, columns, channels)
    full_first, full_second = (
        lax.all_gather(w_first, "wide", axis=0, tiled=True),
        lax.all_gather(w_second, "wide", axis=0, tiled=True),
    )
    kernel_first = full_first.reshape(3, 3, 3, channels, channels)
    kernel_second = full_second.reshape(3, 3, 3, channels, channels)
    tile_wide = tile.astype(jnp.float32)
    first = jax.nn.silu(tile_wide).astype(jnp.bfloat16)
    first_ext = with_halo(first, (("rows", 1),), 1)
    act = conv_forward(first_ext, kernel_first).astype(jnp.bfloat16)
    second = jax.nn.silu(act.astype(jnp.float32)).astype(jnp.bfloat16)
    second_ext = with_halo(second, (("rows", 1),), 1)
    block_out = (tile_wide + conv_forward(second_ext, kernel_second)).astype(jnp.bfloat16)
    live = (jnp.arange(frames, dtype=jnp.int32) < lengths[0])[:, None, None, None]
    out_grad = jnp.where(live, cot[0], jnp.zeros_like(cot[0]))
    out_grad_ext = with_halo(out_grad, (("rows", 1),), 1)
    weight_second = conv_weight_grad(second_ext, out_grad)
    hidden_grad = conv_data_grad(out_grad_ext, kernel_second)
    act_grad = (hidden_grad * silu_slope(act.astype(jnp.float32))).astype(jnp.bfloat16)
    act_grad_ext = with_halo(act_grad, (("rows", 1),), 1)
    weight_first = conv_weight_grad(first_ext, act_grad)
    first_grad = conv_data_grad(act_grad_ext, kernel_first)
    grad_input = (out_grad.astype(jnp.float32) + first_grad * silu_slope(tile_wide)).astype(
        jnp.bfloat16
    )
    scale = 1.0 / math.sqrt(frames * band_rows * columns * band_count * wide_size)
    weight_first = weight_first * scale
    weight_second = weight_second * scale
    total_first, total_second = (
        lax.psum(weight_first.astype(jnp.bfloat16), "rows").astype(jnp.float32),
        lax.psum(weight_second.astype(jnp.bfloat16), "rows").astype(jnp.float32),
    )
    share_first, share_second = (
        lax.psum_scatter(total_first, "wide", scatter_dimension=0, tiled=True),
        lax.psum_scatter(total_second, "wide", scatter_dimension=0, tiled=True),
    )
    return (block_out[None], grad_input[None], share_first, share_second)


def whole(count):
    return [pl.BlockSpec(memory_space=pltpu.VMEM)] * count


def scalars(count):
    return [pl.BlockSpec(memory_space=pltpu.SMEM)] * count


def position(side):
    core = lax.axis_index("rows")
    wide = lax.axis_index("wide")
    high, low = wide // side, lax.rem(wide, side)
    return core, high, low


def walk(core, high, low):
    return jnp.where(core == 0, high, low), jnp.where(core == 0, low, high)


def chip_of(core, p, q, side):
    high, low = walk(core, p, q)
    return high * side + low


def block_rows(share):
    return -(-(share + 8) // 16) * 16


def pack_kernel(dest_ref, pos_ref, slabs_hbm, first_hbm, second_hbm, *refs):
    side = len(refs) - 4
    out_refs = refs[:side]
    slabs_ref, own_ref, block_ref, sem = refs[side:]
    core, high, low = position(side)
    p, _ = walk(core, high, low)
    count, columns, channels = slabs_ref.shape
    share = own_ref.shape[0]
    base = block_rows(share)
    load_slabs = pltpu.make_async_copy(slabs_hbm, slabs_ref, sem.at[0])
    load_first = pltpu.make_async_copy(first_hbm, own_ref, sem.at[1])
    load_second = pltpu.make_async_copy(second_hbm, own_ref, sem.at[1])
    load_slabs.start()

    @pl.when(core == 0)
    def _():
        load_first.start()

    @pl.when(core != 0)
    def _():
        load_second.start()

    block_ref[...] = jnp.zeros(block_ref.shape, BF16)
    row = lax.broadcasted_iota(jnp.int32, (base - share, channels), 0)
    labels = [jnp.full((base - share, channels), -1.0, F32) for _ in range(side)]
    steps, slots = [], []
    for s in range(count):
        p_to, q_to = walk(core, dest_ref[s] // side, lax.rem(dest_ref[s], side))
        steps.append(jnp.bitwise_xor(p, p_to))
        slots.append(q_to)
        place = pos_ref[s].astype(F32)
        for k in range(side):
            hit = jnp.where(steps[s] == k, q_to, -1)
            labels[k] = jnp.where(row == hit, place, labels[k])
    load_slabs.wait()
    for s in range(count):
        start = pl.multiple_of(slots[s] * columns, columns)
        block_ref[steps[s], pl.ds(start, columns), :] = slabs_ref[s]
    for k in range(side):
        out_refs[k][base:, :] = block_ref[k]
    load_first.wait()
    own = own_ref[...].astype(F32)
    for k in range(side):
        out_refs[k][:base, :] = jnp.concatenate([own, labels[k]], axis=0).astype(BF16)


def pack(dest, pos, slabs, first, second, side):
    count, columns, channels = slabs.shape
    rows = block_rows(first.shape[0]) + side * columns
    return pl.pallas_call(
        pack_kernel,
        out_shape=[jax.ShapeDtypeStruct((rows, channels), BF16)] * side,
        in_specs=scalars(2) + [pl.BlockSpec(memory_space=pltpu.HBM)] * 3,
        out_specs=whole(side),
        scratch_shapes=[
            pltpu.VMEM(slabs.shape, BF16),
            pltpu.VMEM(first.shape, BF16),
            pltpu.VMEM((side, side * columns, channels), BF16),
            pltpu.SemaphoreType.DMA((2,)),
        ],
    )(dest, pos, slabs, first, second)


def keep_kernel(*refs):
    half = len(refs) // 2
    for source, target in zip(refs[:half], refs[half:]):
        target[...] = source[...]


def keep(*blocks):
    return pl.pallas_call(
        keep_kernel,
        out_shape=[jax.ShapeDtypeStruct(block.shape, block.dtype) for block in blocks],
        in_specs=whole(len(blocks)),
        out_specs=whole(len(blocks)),
        compiler_params=SMALL,
    )(*blocks)


def relay_kernel(cot_ref, *refs, columns, base):
    side = len(refs) // 2
    ins, outs = refs[:side][::-1], refs[side:]
    core, high, low = position(side)
    _, q = walk(core, high, low)
    for j in range(side):
        start = pl.multiple_of(base + jnp.bitwise_xor(q, j) * columns, 16)
        for k in range(side):
            outs[j][k * base : (k + 1) * base, :] = ins[k][:base, :]
            at = side * base + k * columns
            outs[j][at : at + columns, :] = ins[k][pl.ds(start, columns), :]
    outs[0][side * (base + columns) :, :] = cot_ref[...].reshape(-1, cot_ref.shape[-1])


def relay(cot, ins, columns, base):
    side = len(ins)
    channels = ins[0].shape[1]
    rows = side * (base + columns)
    extra = cot.size // channels
    return pl.pallas_call(
        functools.partial(relay_kernel, columns=columns, base=base),
        out_shape=[jax.ShapeDtypeStruct((rows + extra, channels), BF16)]
        + [jax.ShapeDtypeStruct((rows, channels), BF16)] * (side - 1),
        in_specs=whole(side + 1),
        out_specs=whole(side),
        compiler_params=SMALL,
    )(cot, *ins[::-1])


def settle(blocks, tile_ref, first_row, q, share):
    side = len(blocks)
    base = block_rows(share)
    frames, _, columns, channels = tile_ref.shape
    row = lax.broadcasted_iota(jnp.int32, (base - share, channels), 0)
    slots = []
    for block in blocks:
        for k in range(side):
            labels = block[k * base : (k + 1) * base, :].astype(F32)[share:]
            label = jnp.sum(jnp.where(row == q, labels, 0.0), axis=0, keepdims=True)
            label = jnp.broadcast_to(label, (columns, channels)).astype(BF16)
            at = side * base + k * columns
            slots.append((label, block[at : at + columns, :]))
    for place in range(frames * 2):
        total = jnp.zeros((columns, channels), BF16)
        for label, values in slots:
            total = jnp.where(label == BF16(place), values, total)
        tile_ref[place // 2, first_row + place % 2] = total.astype(F32)


def gather_weight(blocks, wide_ref, core, high, low, share, base):
    side = len(blocks)
    p, q = walk(core, high, low)
    for j in range(side):
        for k in range(side):
            owner = chip_of(core, jnp.bitwise_xor(p, k), jnp.bitwise_xor(q, j), side)
            start = pl.multiple_of(owner * share, 8)
            values = blocks[j][k * base : (k + 1) * base, :].astype(F32)
            wide_ref[pl.ds(start, share), :] = values[:share]


def shifted(field):
    shape = field.shape
    column = lax.broadcasted_iota(jnp.int32, shape, len(shape) - 2)
    count = shape[-2]
    flat = field.reshape(-1, shape[-1])
    low = pltpu.roll(flat, 1, 0).reshape(shape)
    high = pltpu.roll(flat, flat.shape[0] - 1, 0).reshape(shape)
    low = jnp.where(column == 0, 0.0, low)
    high = jnp.where(column == count - 1, 0.0, high)
    return low.astype(BF16), field.astype(BF16), high.astype(BF16)


def spread(field, store, flip):
    rows = field.shape[1]
    columns = shifted(field)
    for b in range(3):
        for e in range(3):
            source = columns[2 - e] if flip else columns[e]
            offset = (1 - b) if flip else (b - 1)
            low = max(0, -offset)
            high = min(rows, rows - offset)
            piece = b * 3 + e
            store(low, high, piece, source[:, low + offset : high + offset])
            for row in range(rows):
                if not low <= row < high:
                    store(row, row + 1, piece, jnp.zeros_like(source[:, :1]))


def store_pieces(columns_ref):
    channels = columns_ref.shape[-1] // 9

    def store(low, high, piece, values):
        columns_ref[:, low:high, :, piece * channels : (piece + 1) * channels] = values

    return store


def spread_weight(wide_ref, out_ref, transposed):
    channels = wide_ref.shape[-1]
    for a in range(3):
        for piece in range(9):
            at = (a * 9 + piece) * channels
            values = wide_ref[at : at + channels, :].astype(BF16)
            frame = slice(a * channels, (a + 1) * channels)
            place = slice(piece * channels, (piece + 1) * channels)
            if transposed:
                out_ref[frame, place] = values
            else:
                out_ref[place, frame] = values


def conv(columns, w_ref, frames):
    channels = w_ref.shape[1] // 3
    product = jnp.dot(columns, w_ref[...], preferred_element_type=F32)
    product = product.reshape(frames, -1, 3 * channels)
    parts = [product[:, :, a * channels : (a + 1) * channels] for a in range(3)]
    out = []
    for t in range(frames):
        out.append(parts[0][max(t - 2, 0)] + parts[1][max(t - 1, 0)] + parts[2][t])
    return out


def conv_back(columns, wl_ref, frames):
    channels = wl_ref.shape[0] // 3
    nt = (((1,), (1,)), ((), ()))
    product = lax.dot_general(columns, wl_ref[...], nt, preferred_element_type=F32)
    product = product.reshape(frames, -1, 3 * channels)
    parts = [product[:, :, a * channels : (a + 1) * channels] for a in range(3)]
    out = []
    for t in range(frames):
        total = parts[2][t]
        for a in range(2):
            for source in range(frames):
                if max(source + a - 2, 0) == t:
                    total = total + parts[a][source]
        out.append(total)
    return out


def act_gradient(act, wl_ref, columns_ref, store):
    frames, rows, count, nine = columns_ref.shape
    hidden = conv_back(columns_ref[...].reshape(-1, nine), wl_ref, frames)
    for t in range(frames):
        value = act[t].astype(F32)
        sig = 1.0 / (1.0 + jnp.exp(-value))
        slope = sig * (1.0 + value * (1.0 - sig))
        store(t, (hidden[t].reshape(value.shape) * slope).astype(BF16))


def spread_chosen(of_core_zero, mine_ref, other_ref, out_ref, transposed):
    core = lax.axis_index("rows")
    own = (core == 0) if of_core_zero else (core != 0)

    @pl.when(own)
    def _():
        spread_weight(mine_ref, out_ref, transposed)

    @pl.when(jnp.logical_not(own))
    def _():
        spread_weight(other_ref, out_ref, transposed)


def prepare_kernel(length_ref, *refs, share):
    side = len(refs) - 5
    blocks, first_other = refs[:side], refs[side]
    tile_ref, wide_ref, out_grad_ref, columns_ref = refs[side + 1 :]
    core, high, low = position(side)
    frames, rows, columns, channels = out_grad_ref.shape
    band_rows = rows // 2
    _, q = walk(core, high, low)
    settle(blocks, tile_ref, 0, q, share)
    gather_weight(blocks, wide_ref, core, high, low, share, block_rows(share))
    end = side * (block_rows(share) + columns)
    band = (frames, band_rows, columns, channels)
    for block, owner in ((blocks[0], core), (first_other, 1 - core)):
        cot = block[end:, :].reshape(band)
        for t in range(frames):
            out_grad_ref[t, pl.ds(owner * band_rows, band_rows)] = jnp.where(
                t < length_ref[0], cot[t].astype(F32), 0.0
            ).astype(BF16)

    @pl.when(core == 0)
    def _():
        spread(out_grad_ref[...].astype(F32), store_pieces(columns_ref), True)


def prepare(length, blocks_mine, first_other, band, share):
    frames, band_rows, columns, channels = band
    field = (frames, 2 * band_rows, columns, channels)
    return pl.pallas_call(
        functools.partial(prepare_kernel, share=share),
        out_shape=[
            jax.ShapeDtypeStruct(band, F32),
            jax.ShapeDtypeStruct((27 * channels, channels), F32),
            jax.ShapeDtypeStruct(field, BF16),
            jax.ShapeDtypeStruct(field[:-1] + (9 * channels,), BF16),
        ],
        in_specs=scalars(1) + whole(len(blocks_mine) + 1),
        out_specs=whole(4),
        compiler_params=SMALL,
    )(length, *blocks_mine, first_other)


def unit_kernel(tile_mine, wide_mine, out_grad_ref, columns_ref, *refs, scale, side, share):
    blocks_other, refs = refs[:side], refs[side:]
    tile_ref, act_ref, act_grad_ref, wide_other = refs[:4]
    outs, refs = refs[4 : 4 + side], refs[4 + side :]
    w_ref, wl_ref, total_ref, x_scratch, right_ref = refs
    core, high, low = position(side)
    frames, rows, columns, channels = tile_ref.shape
    band_rows = rows // 2
    cells = frames * rows * columns
    nine = 9 * channels

    _, other_q = walk(1 - core, high, low)
    settle(blocks_other, tile_ref, (1 - core) * band_rows, other_q, share)
    tile_ref[:, pl.ds(core * band_rows, band_rows)] = tile_mine[...]
    gather_weight(blocks_other, wide_other, 1 - core, high, low, share, block_rows(share))
    spread_chosen(True, wide_mine, wide_other, w_ref, False)

    tile = tile_ref[...]
    first = tile / (1.0 + jnp.exp(-tile))
    spread(first, store_pieces(x_scratch.at[0]), False)
    act = conv(x_scratch[0].reshape(cells, nine), w_ref, frames)
    for t in range(frames):
        act_ref[t] = act[t].astype(BF16).reshape(rows, columns, channels)
    act = act_ref[...].astype(F32)
    second = act / (1.0 + jnp.exp(-act))
    spread(second, store_pieces(x_scratch.at[1]), False)

    @pl.when(core == 0)
    def _():
        def store(t, values):
            act_grad_ref[t] = values

        spread_weight(wide_other, wl_ref, True)
        act_gradient(act_ref, wl_ref, columns_ref, store)

    upstream = jnp.where(core == 0, act_grad_ref[...].astype(F32), out_grad_ref[...].astype(F32))
    upstream = upstream.reshape(frames, rows * columns, channels)
    for a in range(3):
        for t in range(frames):
            met = [upstream[s] for s in range(frames) if max(s + a - 2, 0) == t]
            met = sum(met[1:], met[0]) if met else jnp.zeros_like(upstream[0])
            frame = slice(a * channels, (a + 1) * channels)
            right_ref[t * rows * columns : (t + 1) * rows * columns, frame] = met.astype(BF16)
    product = lax.dot_general(
        x_scratch[core].reshape(cells, nine),
        right_ref[...],
        (((0,), (0,)), ((), ())),
        preferred_element_type=F32,
    )
    for a in range(3):
        for piece in range(9):
            at = (a * 9 + piece) * channels
            place = slice(piece * channels, (piece + 1) * channels)
            block = product[place, a * channels : (a + 1) * channels]
            total_ref[at : at + channels, :] = block * scale
    p, q = walk(core, high, low)
    for k in range(side):
        for j in range(side):
            owner = chip_of(core, j, jnp.bitwise_xor(q, k), side)
            start = pl.multiple_of(owner * share, 8)
            outs[k][j] = total_ref[pl.ds(start, share), :].astype(BF16)


def unit(prepared, blocks_other, scale, share):
    frames, rows, columns, channels = prepared[2].shape
    side = len(blocks_other)
    field = (frames, rows, columns, channels)
    cells = frames * rows * columns
    part = jax.ShapeDtypeStruct((side, share, channels), BF16)
    flops = 2 * 27 * channels * channels * cells * 3
    outs = pl.pallas_call(
        functools.partial(unit_kernel, scale=scale, side=side, share=share),
        out_shape=[
            jax.ShapeDtypeStruct(field, F32),
            jax.ShapeDtypeStruct(field, BF16),
            jax.ShapeDtypeStruct(field, BF16),
            jax.ShapeDtypeStruct((27 * channels, channels), F32),
        ]
        + [part] * side,
        in_specs=whole(len(prepared) + side),
        out_specs=whole(4 + side),
        scratch_shapes=[
            pltpu.VMEM((9 * channels, 3 * channels), BF16),
            pltpu.VMEM((3 * channels, 9 * channels), BF16),
            pltpu.VMEM((27 * channels, channels), F32),
            pltpu.VMEM((2, frames, rows, columns, 9 * channels), BF16),
            pltpu.VMEM((cells, 3 * channels), BF16),
        ],
        compiler_params=pltpu.CompilerParams(vmem_limit_bytes=32 * 1024 * 1024),
        cost_estimate=pl.CostEstimate(flops=flops, bytes_accessed=4_000_000, transcendentals=0),
    )(*prepared, *blocks_other)
    tile, act, act_grad, wide_other = outs[:4]
    return (tile, act, prepared[2], act_grad, prepared[1], wide_other), outs[4:]


def finish_kernel(
    tile_ref,
    act_ref,
    out_grad_ref,
    act_grad_ref,
    wide_mine,
    wide_other,
    block_ref,
    grad_ref,
    w_ref,
    wl_ref,
    columns_ref,
    up_ref,
):
    frames, band_rows, columns, channels = block_ref.shape
    nine = 9 * channels
    core = lax.axis_index("rows")
    mine = pl.ds(core * band_rows, band_rows)
    shape = (band_rows, columns, channels)

    act = act_ref[...].astype(F32)
    second = act / (1.0 + jnp.exp(-act))
    spread(second, store_pieces(columns_ref), False)
    spread_chosen(False, wide_mine, wide_other, w_ref, False)
    out = conv(columns_ref[:, mine].reshape(-1, nine), w_ref, frames)
    for t in range(frames):
        block_ref[t] = (tile_ref[t, mine] + out[t].reshape(shape)).astype(BF16)

    @pl.when(core == 0)
    def _():
        up_ref[...] = act_grad_ref[...]

    @pl.when(core != 0)
    def _():
        def store(t, values):
            up_ref[t] = values

        spread_weight(wide_mine, wl_ref, True)
        spread(out_grad_ref[...].astype(F32), store_pieces(columns_ref), True)
        act_gradient(act_ref, wl_ref, columns_ref, store)

    spread(up_ref[...].astype(F32), store_pieces(columns_ref), True)
    spread_chosen(True, wide_mine, wide_other, wl_ref, True)
    out = conv_back(columns_ref[:, mine].reshape(-1, nine), wl_ref, frames)
    for t in range(frames):
        tile = tile_ref[t, mine]
        sig = 1.0 / (1.0 + jnp.exp(-tile))
        slope = sig * (1.0 + tile * (1.0 - sig))
        upstream = out_grad_ref[t, mine].astype(F32)
        grad_ref[t] = (upstream + out[t].reshape(shape) * slope).astype(BF16)


def finish(kept):
    frames, rows, columns, channels = kept[0].shape
    band = jax.ShapeDtypeStruct((frames, rows // 2, columns, channels), BF16)
    flops = 2 * 27 * channels * channels * frames * rows * columns
    return pl.pallas_call(
        finish_kernel,
        out_shape=[band] * 2,
        in_specs=whole(len(kept)),
        out_specs=whole(2),
        scratch_shapes=[
            pltpu.VMEM((9 * channels, 3 * channels), BF16),
            pltpu.VMEM((3 * channels, 9 * channels), BF16),
            pltpu.VMEM((frames, rows, columns, 9 * channels), BF16),
            pltpu.VMEM((frames, rows, columns, channels), BF16),
        ],
        compiler_params=pltpu.CompilerParams(vmem_limit_bytes=20 * 1024 * 1024),
        cost_estimate=pl.CostEstimate(flops=flops, bytes_accessed=2_000_000, transcendentals=0),
    )(*kept)


def total_of(refs, at):
    total = refs[0][at].astype(F32)
    for ref in refs[1:]:
        total = total + ref[at].astype(F32)
    return total


def middle_kernel(*refs):
    side = len(refs) // 2
    core, high, low = position(side)
    p, _ = walk(core, high, low)
    for k in range(side):
        refs[side + k][...] = total_of(refs[:side][::-1], jnp.bitwise_xor(p, k)).astype(BF16)


def middle(parts):
    side = len(parts)
    return pl.pallas_call(
        middle_kernel,
        out_shape=[jax.ShapeDtypeStruct(parts[0].shape[1:], BF16)] * side,
        in_specs=whole(side),
        out_specs=whole(side),
        compiler_params=SMALL,
    )(*parts[::-1])


def last_kernel(*refs):
    refs[-1][...] = total_of(refs[:-1][::-1], ...)


def last(parts):
    return pl.pallas_call(
        last_kernel,
        out_shape=jax.ShapeDtypeStruct(parts[0].shape, F32),
        in_specs=whole(len(parts)),
        out_specs=whole(1)[0],
        compiler_params=SMALL,
    )(*parts[::-1])


def body_pair(slabs, dest, pos, lengths, cot, w_first, w_second):
    wide_size = lax.axis_size("wide")
    side = math.isqrt(wide_size)
    core = lax.axis_index("rows")
    frames, band_rows, columns, channels = cot.shape[1:]
    share = w_first.shape[0]
    base = block_rows(share)

    def exchange(block):
        return lax.ppermute(block, "rows", [(0, 1), (1, 0)])

    def pairs(axes, k):
        both = []
        for chip in range(wide_size):
            high, low = chip // side, chip % side
            targets = ((high ^ k) * side + low, high * side + (low ^ k))
            both += [(chip * 2 + c, targets[axes[c]] * 2 + c) for c in range(2)]
        return both

    def send(blocks, axes):
        sent = [
            lax.ppermute(blocks[k], ("wide", "rows"), pairs(axes, k))
            for k in range(side - 1, 0, -1)
        ]
        return [blocks[0]] + sent[::-1]

    packed = pack(dest[0, 0], pos[0, 0], slabs[0, 0], w_first, w_second, side)
    _, *arrived = send(packed, (0, 1))
    kept_block, kept_cot = keep(packed[0], cot[0])
    relayed = relay(kept_cot, [kept_block, *arrived], columns, base)
    blocks_mine = send(relayed, (1, 0))
    own_block, _ = lax.optimization_barrier((blocks_mine[0], blocks_mine[2]))
    blocks_other = [exchange(block) for block in (own_block, *blocks_mine[1:])]

    scale = 1.0 / math.sqrt(frames * band_rows * columns * 2 * wide_size)
    prepared = prepare(lengths, blocks_mine, blocks_other[0], cot.shape[1:], share)
    kept, parts = unit(prepared, blocks_other, scale, share)
    block_out, grad_input = finish(kept)

    arrived = send(parts, (1, 0))
    *arrived, block_out, grad_input = lax.optimization_barrier((*arrived, block_out, grad_input))
    total = last(send(middle(arrived), (0, 1)))
    total_other = exchange(total)
    share_first = jnp.where(core == 0, total, total_other)
    share_second = jnp.where(core == 0, total_other, total)
    return (block_out[None], grad_input[None], share_first, share_second)


def solution(mesh):
    side = math.isqrt(mesh.shape["wide"])
    square = side * side == mesh.shape["wide"] and side & (side - 1) == 0
    body = body_pair if mesh.shape["rows"] == 2 and square else body_general
    return jax.shard_map(
        body,
        mesh=mesh,
        in_specs=(
            P("wide", "rows", None, None, None),
            P("wide", "rows", None),
            P("wide", "rows", None),
            P("wide"),
            P("wide", None, "rows", None, None),
            P("wide", None),
            P("wide", None),
        ),
        out_specs=(
            P("wide", None, "rows", None, None),
            P("wide", None, "rows", None, None),
            P("wide", None),
            P("wide", None),
        ),
        check_vma=False,
    )
```
